512 devices in a mesh: dp: 2 (over y_hi), inp: 8 (over x, core), out: 8 (over z), dep: 4 (over y_lo).
Axes of the slice: x: 4, y: 8 (y_hi: 2, y_lo: 4; y = y_hi * 4 + y_lo), z: 8, core: 2. Of those that a mesh axis runs over, the one named last changes fastest.
Arguments:
- tokens: bfloat16 [2, 128, 8192], P('dp', ('inp', 'out'), 'dep'), may hold values from -6 to 6
- gate_weight: bfloat16 [8192, 32768], P('dep', ('dp', 'inp', 'out')), may hold values from -0.0625 to 0.0625
- up_weight: bfloat16 [8192, 32768], P('dep', ('dp', 'inp', 'out')), may hold values from -0.0625 to 0.0625
- cotangent: bfloat16 [2, 128, 32768], P(None, 'dep', ('dp', 'inp', 'out')), may hold values from -1.5 to 1.5
Outputs:
- hidden: bfloat16 [2, 128, 32768], P(None, 'dep', ('dp', 'inp', 'out'))
- input_grad: bfloat16 [2, 128, 8192], P('dp', ('inp', 'out'), 'dep')
- gate_grad: bfloat16 [8192, 32768], P('dep', ('dp', 'inp', 'out'))
- up_grad: bfloat16 [8192, 32768], P('dep', ('dp', 'inp', 'out'))
The draws below stay inside these ranges and needn't reach their ends.
All inputs are finite; a program needn't handle non-finite values.
Results may differ from the reference program's by a relative error of at most 0.0049.
Values may be sent and summed in bfloat16 or wider, within the bound.
No kernel may reach another device: no remote copies, remote signals or barrier semaphores. Data moves between devices by JAX's collectives and lax.ppermute only.
A program may use at most 64 MiB of HBM per device.

```python
import jax
import jax.numpy as jnp

D = 8192
FF = 32768
TOK = 128
MB = 2


def block_scale(own_key, dims, shards, smallest, largest):
    def one(position, blocks):
        heights = jax.random.uniform(jax.random.fold_in(jax.random.fold_in(own_key, 6), position), (blocks,), jnp.float32, smallest / len(shards), largest / len(shards))
        return jnp.repeat(jnp.exp(heights), dims[position] // blocks).reshape((-1,) + (1,) * (len(dims) - position - 1))

    factor_of = one(*shards[0])
    for cut in shards[1:]:
        factor_of = factor_of * one(*cut)
    return factor_of


def bell_draw(own_key, dims, deviation, most, pieces=(), dtype=jnp.bfloat16):
    factor_of = block_scale(own_key, dims, pieces, -0.22, 0.18) if pieces else 1.0
    drawn = jax.random.normal(own_key, dims, jnp.float32) * deviation * factor_of
    return jnp.minimum(jnp.maximum(drawn, -most), most).astype(dtype)


def setup_inputs(seed: int = 0) -> dict:
    keys = jax.random.split(jax.random.key(seed), 5)
    tokens = bell_draw(keys[0], (MB, TOK, D), 1.0, 6.0, ((0, 2), (1, 64), (2, 4)))
    gate_weight = bell_draw(keys[1], (D, FF), D ** -0.5, 0.0625, ((0, 4), (1, 128)))
    up_weight = bell_draw(keys[2], (D, FF), D ** -0.5, 0.0625, ((0, 4), (1, 128)))
    cotangent = bell_draw(keys[3], (MB, TOK, FF), 0.25, 1.5, ((1, 4), (2, 128)))
    return {"tokens": tokens, "gate_weight": gate_weight, "up_weight": up_weight, "cotangent": cotangent}


def reference(tokens, gate_weight, up_weight, cotangent):
    batches = tokens.shape[0]
    flat_tokens = tokens.reshape(-1, tokens.shape[2])
    gate_vals = jnp.dot(flat_tokens, gate_weight, preferred_element_type=jnp.float32)
    up_vals = jnp.dot(flat_tokens, up_weight, preferred_element_type=jnp.float32)
    sig_gate = jax.nn.sigmoid(gate_vals)
    silu_gate = gate_vals * sig_gate
    hidden = (silu_gate * up_vals).astype(jnp.bfloat16)
    cot_vals = cotangent.reshape(-1, cotangent.shape[2]).astype(jnp.float32)
    d_gate = (cot_vals * up_vals * sig_gate * (1.0 + gate_vals * (1.0 - sig_gate))).astype(jnp.bfloat16)
    d_up = (cot_vals * silu_gate).astype(jnp.bfloat16)
    input_grad = jnp.dot(d_gate, gate_weight.T, preferred_element_type=jnp.float32)
    input_grad = input_grad + jnp.dot(d_up, up_weight.T, preferred_element_type=jnp.float32)
    gate_grad = jnp.dot(flat_tokens.T, d_gate, preferred_element_type=jnp.float32)
    up_grad = jnp.dot(flat_tokens.T, d_up, preferred_element_type=jnp.float32)
    return (hidden.reshape(batches, -1, hidden.shape[1]),
            input_grad.astype(jnp.bfloat16).reshape(tokens.shape),
            gate_grad.astype(jnp.bfloat16),
            up_grad.astype(jnp.bfloat16))
```

```python
import jax
import jax.numpy as jnp
import numpy as np
from jax import lax
from jax.sharding import Mesh, PartitionSpec as P

F32 = jnp.float32
BF16 = jnp.bfloat16
CHIPS = ("x", "dp", "out")


def per_device(tokens, gate_weight, up_weight, cotangent):
    rows, feature = tokens.shape[1], tokens.shape[2]
    units = gate_weight.shape[1]
    quarters = lax.axis_size("dep")
    micro = lax.axis_size("dp")
    lanes = lax.axis_size("out") * rows
    peers = lax.axis_size("x") * micro * lax.axis_size("out")
    core = lax.axis_index("core")
    swap = ((0, 1), (1, 0))

    own_tokens = lax.all_to_all(
        jnp.broadcast_to(tokens, (peers, rows, feature)), CHIPS, 0, 0, tiled=True
    ).reshape(-1, feature)
    other_tokens = lax.ppermute(own_tokens, "core", swap)
    halves = (own_tokens, other_tokens)

    partial = jnp.stack(
        [
            jnp.dot(half, weight, preferred_element_type=F32)
            .astype(BF16)
            .reshape(quarters, -1, units)
            for weight in (gate_weight, up_weight)
            for half in halves
        ],
        axis=1,
    )
    received = lax.all_to_all(partial, "dep", 0, 0, tiled=True)
    summed = jnp.sum(received.astype(F32), axis=0).reshape(2, 2, micro, lanes, units)
    gate_vals, up_vals = summed[0], summed[1]

    sig_gate = jax.nn.sigmoid(gate_vals)
    silu_gate = gate_vals * sig_gate
    hidden = (silu_gate * up_vals).astype(BF16)
    cot = cotangent.reshape(micro, 2, lanes, units)
    cot_even, cot_odd = cot[:, 0], cot[:, 1]
    first = core == 0
    cot_vals = jnp.stack(
        [jnp.where(first, cot_even, cot_odd), jnp.where(first, cot_odd, cot_even)]
    ).astype(F32)
    d_gate = (cot_vals * up_vals * sig_gate * (1.0 + gate_vals * (1.0 - sig_gate))).astype(BF16)
    d_up = (cot_vals * silu_gate).astype(BF16)

    mine = jnp.stack([d_gate, d_up]).reshape(1, 4, micro * lanes, units)
    full = lax.all_to_all(
        jnp.broadcast_to(mine, (quarters,) + mine.shape[1:]), "dep", 0, 0, tiled=True
    )
    gate_own, gate_other, up_own, up_other = (
        full[:, k].reshape(-1, units) for k in range(4)
    )

    def back(gate_half, up_half):
        contract = (((1,), (1,)), ((), ()))
        return lax.dot_general(
            gate_half, gate_weight, contract, preferred_element_type=F32
        ) + lax.dot_general(up_half, up_weight, contract, preferred_element_type=F32)

    arrived = lax.ppermute(back(gate_other, up_other).astype(BF16), "core", swap)
    chip_sum = (back(gate_own, up_own) + arrived.astype(F32)).astype(BF16)
    pieces = lax.all_to_all(chip_sum.reshape(peers, rows, feature), CHIPS, 0, 0, tiled=True)
    input_grad = jnp.sum(pieces.astype(F32), axis=0)

    def grad(own, other):
        contract = (((0,), (0,)), ((), ()))
        return (
            lax.dot_general(own_tokens, own, contract, preferred_element_type=F32)
            + lax.dot_general(other_tokens, other, contract, preferred_element_type=F32)
        ).astype(BF16)

    hid_even = jnp.where(first, hidden[0], hidden[1])
    hid_odd = jnp.where(first, hidden[1], hidden[0])
    return (
        jnp.stack([hid_even, hid_odd], axis=1).reshape(cotangent.shape),
        input_grad.astype(BF16).reshape(tokens.shape),
        grad(gate_own, gate_other),
        grad(up_own, up_other),
    )


def solution(mesh):
    dp, inp, out, dep = (mesh.shape[name] for name in ("dp", "inp", "out", "dep"))
    split = Mesh(
        np.asarray(mesh.devices).reshape(dp, inp // 2, 2, out, dep),
        ("dp", "x", "core", "out", "dep"),
    )
    tokens_at = P("dp", ("x", "core", "out"), "dep")
    weight_at = P("dep", ("dp", "x", "core", "out"))
    hidden_at = P(None, "dep", ("dp", "x", "core", "out"))
    return jax.shard_map(
        per_device,
        mesh=split,
        in_specs=(tokens_at, weight_at, weight_at, hidden_at),
        out_specs=(hidden_at, tokens_at, weight_at, weight_at),
        check_vma=False,
    )
```

```python
import jax
import jax.numpy as jnp
import numpy as np
from jax import lax
from jax.sharding import Mesh, PartitionSpec as P

F32 = jnp.float32
BF16 = jnp.bfloat16
CHIPS = ("x", "dp", "out")


def per_device(tokens, gate_weight, up_weight, cotangent):
    rows, feature = tokens.shape[1], tokens.shape[2]
    units = gate_weight.shape[1]
    quarters = lax.axis_size("dep")
    micro = lax.axis_size("dp")
    lanes = lax.axis_size("out") * rows
    peers = lax.axis_size("x") * micro * lax.axis_size("out")
    first = lax.axis_index("core") == 0

    def swap(block):
        return lax.ppermute(block, "core", ((0, 1), (1, 0)))

    def paired(even, odd):
        return jnp.where(first, even, odd), jnp.where(first, odd, even)

    own_tokens = lax.all_to_all(
        jnp.broadcast_to(tokens, (peers, rows, feature)), CHIPS, 0, 0, tiled=True
    ).reshape(-1, feature)

    weights = jnp.concatenate(
        [gate_weight, swap(gate_weight), up_weight, swap(up_weight)], axis=1
    )
    cot = cotangent.reshape(micro, 2, lanes, units)
    cot_own, cot_sent = paired(cot[:, 0], cot[:, 1])
    cot_vals = jnp.concatenate([cot_own, swap(cot_sent)], axis=2).reshape(-1, 2 * units)
    cot_vals = cot_vals.astype(F32)

    partial = jnp.dot(own_tokens, weights, preferred_element_type=F32).astype(BF16)
    received = lax.all_to_all(
        partial.reshape(quarters, -1, 4 * units), "dep", 0, 0, tiled=True
    )
    summed = jnp.sum(received.astype(F32), axis=0)
    gate_vals, up_vals = summed[:, : 2 * units], summed[:, 2 * units :]

    sig_gate = jax.nn.sigmoid(gate_vals)
    silu_gate = gate_vals * sig_gate
    hidden = (silu_gate * up_vals).astype(BF16).reshape(micro, lanes, 2 * units)
    d_gate = (cot_vals * up_vals * sig_gate * (1.0 + gate_vals * (1.0 - sig_gate))).astype(BF16)
    d_up = (cot_vals * silu_gate).astype(BF16)
    mine = jnp.concatenate([d_gate, d_up], axis=1)
    full = lax.all_to_all(
        jnp.broadcast_to(mine[None], (quarters,) + mine.shape), "dep", 0, 0, tiled=True
    ).reshape(-1, 4 * units)

    chip_sum = lax.dot_general(
        full, weights, (((1,), (1,)), ((), ())), preferred_element_type=F32
    ).astype(BF16)
    pieces = lax.all_to_all(chip_sum.reshape(peers, rows, feature), CHIPS, 0, 0, tiled=True)
    input_grad = jnp.sum(pieces.astype(F32), axis=0)

    other_tokens = swap(own_tokens)
    parts = [full[:, k * units : (k + 1) * units] for k in range(4)]

    def grad(own, sent):
        contract = (((0,), (0,)), ((), ()))
        return (
            lax.dot_general(own_tokens, own, contract, preferred_element_type=F32)
            + lax.dot_general(other_tokens, swap(sent), contract, preferred_element_type=F32)
        ).astype(BF16)

    hid = paired(hidden[:, :, :units], swap(hidden[:, :, units:]))
    return (
        jnp.stack(hid, axis=1).reshape(cotangent.shape),
        input_grad.astype(BF16).reshape(tokens.shape),
        grad(parts[0], parts[1]),
        grad(parts[2], parts[3]),
    )


def solution(mesh):
    dp, inp, out, dep = (mesh.shape[name] for name in ("dp", "inp", "out", "dep"))
    split = Mesh(
        np.asarray(mesh.devices).reshape(dp, inp // 2, 2, out, dep),
        ("dp", "x", "core", "out", "dep"),
    )
    tokens_at = P("dp", ("x", "core", "out"), "dep")
    weight_at = P("dep", ("dp", "x", "core", "out"))
    hidden_at = P(None, "dep", ("dp", "x", "core", "out"))
    return jax.shard_map(
        per_device,
        mesh=split,
        in_specs=(tokens_at, weight_at, weight_at, hidden_at),
        out_specs=(hidden_at, tokens_at, weight_at, weight_at),
        check_vma=False,
    )
```

```python
import jax
import jax.numpy as jnp
import numpy as np
from jax import lax
from jax.sharding import Mesh, PartitionSpec as P

F32 = jnp.float32
BF16 = jnp.bfloat16
CHIPS = ("x", "dp", "out")


def per_device(tokens, gate_weight, up_weight, cotangent):
    rows, feature = tokens.shape[1], tokens.shape[2]
    units = gate_weight.shape[1]
    quarters = lax.axis_size("dep")
    micro = lax.axis_size("dp")
    lanes = lax.axis_size("out") * rows
    peers = lax.axis_size("x") * micro * lax.axis_size("out")
    first = lax.axis_index("core") == 0

    def swap(block):
        return lax.ppermute(block, "core", ((0, 1), (1, 0)))

    def paired(even, odd):
        return jnp.where(first, even, odd), jnp.where(first, odd, even)

    own_tokens = lax.all_to_all(
        jnp.broadcast_to(tokens, (peers, rows, feature)), CHIPS, 0, 0, tiled=True
    ).reshape(-1, feature)

    weights = (gate_weight, swap(gate_weight), up_weight, swap(up_weight))
    cot = cotangent.reshape(micro, 2, lanes, units)
    cot_own, cot_sent = paired(cot[:, 0], cot[:, 1])
    cot_vals = jnp.concatenate([cot_own, swap(cot_sent)], axis=2).reshape(-1, 2 * units)
    cot_vals = cot_vals.astype(F32)

    partial = jnp.concatenate(
        [jnp.dot(own_tokens, w, preferred_element_type=F32).astype(BF16) for w in weights],
        axis=1,
    )
    received = lax.all_to_all(
        partial.reshape(quarters, -1, 4 * units), "dep", 0, 0, tiled=True
    )
    summed = jnp.sum(received.astype(F32), axis=0)
    gate_vals, up_vals = summed[:, : 2 * units], summed[:, 2 * units :]

    sig_gate = jax.nn.sigmoid(gate_vals)
    silu_gate = gate_vals * sig_gate
    hidden = (silu_gate * up_vals).astype(BF16).reshape(micro, lanes, 2 * units)
    d_gate = (cot_vals * up_vals * sig_gate * (1.0 + gate_vals * (1.0 - sig_gate))).astype(BF16)
    d_up = (cot_vals * silu_gate).astype(BF16)
    mine = jnp.concatenate([d_gate, d_up], axis=1)
    full = lax.all_to_all(
        jnp.broadcast_to(mine[None], (quarters,) + mine.shape), "dep", 0, 0, tiled=True
    ).reshape(-1, 4 * units)

    parts = [full[:, k * units : (k + 1) * units] for k in range(4)]
    across = (((1,), (1,)), ((), ()))
    chip_sum = sum(
        lax.dot_general(part, w, across, preferred_element_type=F32)
        for part, w in zip(parts, weights)
    ).astype(BF16)
    blocks = chip_sum.reshape(peers, rows, -1, 128).swapaxes(1, 2)
    pieces = lax.all_to_all(blocks.reshape(peers, -1, 128), CHIPS, 0, 0, tiled=True)
    input_grad = jnp.sum(pieces.astype(F32), axis=0).astype(BF16)
    input_grad = input_grad.reshape(-1, rows, 128).swapaxes(0, 1)

    other_tokens = swap(own_tokens)
    def grad(own, sent):
        contract = (((0,), (0,)), ((), ()))
        return (
            lax.dot_general(own_tokens, own, contract, preferred_element_type=F32)
            + lax.dot_general(other_tokens, swap(sent), contract, preferred_element_type=F32)
        ).astype(BF16)

    hid = paired(hidden[:, :, :units], swap(hidden[:, :, units:]))
    return (
        jnp.stack(hid, axis=1).reshape(cotangent.shape),
        input_grad.reshape(tokens.shape),
        grad(parts[0], parts[1]),
        grad(parts[2], parts[3]),
    )


def solution(mesh):
    dp, inp, out, dep = (mesh.shape[name] for name in ("dp", "inp", "out", "dep"))
    split = Mesh(
        np.asarray(mesh.devices).reshape(dp, inp // 2, 2, out, dep),
        ("dp", "x", "core", "out", "dep"),
    )
    tokens_at = P("dp", ("x", "core", "out"), "dep")
    weight_at = P("dep", ("dp", "x", "core", "out"))
    hidden_at = P(None, "dep", ("dp", "x", "core", "out"))
    return jax.shard_map(
        per_device,
        mesh=split,
        in_specs=(tokens_at, weight_at, weight_at, hidden_at),
        out_specs=(hidden_at, tokens_at, weight_at, weight_at),
        check_vma=False,
    )
```

```python
import jax
import jax.numpy as jnp
import numpy as np
from jax import lax
from jax.sharding import Mesh, PartitionSpec as P

F32 = jnp.float32
BF16 = jnp.bfloat16
PAIR = ((0, 1), (1, 0))
PLANE = ("x", "out")


def spread(block, axes, peers):
    return lax.all_to_all(
        jnp.broadcast_to(block[None], (peers,) + block.shape), axes, 0, 0, tiled=True
    )


def per_device(tokens, gate_weight, up_weight, cotangent):
    rows, feature = tokens.shape[1], tokens.shape[2]
    units = gate_weight.shape[1]
    quarters = lax.axis_size("dep")
    micro = lax.axis_size("dp")
    lanes = lax.axis_size("out") * rows
    peers = lax.axis_size("x") * lax.axis_size("out")
    core = lax.axis_index("core") == 0
    group = lax.axis_index("dp") == 0

    def swap(block):
        return lax.ppermute(block, "core", PAIR)

    def paired(which, even, odd):
        return jnp.where(which, even, odd), jnp.where(which, odd, even)

    crossed = lax.ppermute(tokens[0], "dp", PAIR)
    near = spread(tokens[0], PLANE, peers).reshape(-1, feature)
    far = spread(crossed, PLANE, peers).reshape(-1, feature)

    weights = (gate_weight, swap(gate_weight), up_weight, swap(up_weight))
    cot = cotangent.reshape(micro, 2, lanes, units)
    cot_own, cot_sent = paired(core, cot[:, 0], cot[:, 1])
    cot_vals = jnp.concatenate([cot_own, swap(cot_sent)], axis=2)
    cot_vals = jnp.concatenate(paired(group, cot_vals[0], cot_vals[1]), axis=0).astype(F32)

    def forward(half):
        vals = [jnp.dot(half, w, preferred_element_type=F32).astype(BF16) for w in weights]
        return jnp.concatenate(vals, axis=1).reshape(quarters, lanes, 4 * units)

    partial = jnp.concatenate([forward(near), forward(far)], axis=1)
    received = lax.all_to_all(partial, "dep", 0, 0, tiled=True)
    summed = jnp.sum(received.astype(F32), axis=0)
    gate_vals, up_vals = summed[:, : 2 * units], summed[:, 2 * units :]

    sig_gate = jax.nn.sigmoid(gate_vals)
    silu_gate = gate_vals * sig_gate
    hidden = (silu_gate * up_vals).astype(BF16).reshape(micro, lanes, 2 * units)
    d_gate = (cot_vals * up_vals * sig_gate * (1.0 + gate_vals * (1.0 - sig_gate))).astype(BF16)
    d_up = (cot_vals * silu_gate).astype(BF16)
    full = spread(jnp.concatenate([d_gate, d_up], axis=1), "dep", quarters)
    full = full.reshape(quarters, micro, lanes, 4 * units)
    near_d = full[:, 0].reshape(-1, 4 * units)
    far_d = full[:, 1].reshape(-1, 4 * units)

    def back(half):
        across = (((1,), (1,)), ((), ()))
        total = sum(
            lax.dot_general(
                half[:, k * units : (k + 1) * units], w, across, preferred_element_type=F32
            )
            for k, w in enumerate(weights)
        ).astype(BF16)
        blocks = total.reshape(peers, rows, -1, 128).swapaxes(1, 2)
        pieces = lax.all_to_all(blocks.reshape(peers, -1, 128), PLANE, 0, 0, tiled=True)
        return jnp.sum(pieces.astype(F32), axis=0)

    arrived = lax.ppermute(back(far_d), "dp", PAIR)
    input_grad = (back(near_d) + arrived).astype(BF16)
    input_grad = input_grad.reshape(-1, rows, 128).swapaxes(0, 1)

    own_tokens = jnp.concatenate([near, far], axis=0)
    other_tokens = swap(own_tokens)

    def grad(k):
        own, sent = (
            jnp.concatenate(
                [half[:, j * units : (j + 1) * units] for half in (near_d, far_d)], axis=0
            )
            for j in (k, k + 1)
        )
        contract = (((0,), (0,)), ((), ()))
        return (
            lax.dot_general(own_tokens, own, contract, preferred_element_type=F32)
            + lax.dot_general(other_tokens, swap(sent), contract, preferred_element_type=F32)
        ).astype(BF16)

    hid = jnp.stack(paired(core, hidden[:, :, :units], swap(hidden[:, :, units:])), axis=1)
    hid = jnp.stack(paired(group, hid[0], hid[1]))
    return (
        hid.reshape(cotangent.shape),
        input_grad.reshape(tokens.shape),
        grad(0),
        grad(2),
    )


def solution(mesh):
    dp, inp, out, dep = (mesh.shape[name] for name in ("dp", "inp", "out", "dep"))
    split = Mesh(
        np.asarray(mesh.devices).reshape(dp, inp // 2, 2, out, dep),
        ("dp", "x", "core", "out", "dep"),
    )
    tokens_at = P("dp", ("x", "core", "out"), "dep")
    weight_at = P("dep", ("dp", "x", "core", "out"))
    hidden_at = P(None, "dep", ("dp", "x", "core", "out"))
    return jax.shard_map(
        per_device,
        mesh=split,
        in_specs=(tokens_at, weight_at, weight_at, hidden_at),
        out_specs=(hidden_at, tokens_at, weight_at, weight_at),
        check_vma=False,
    )
```

```python
import jax
import jax.numpy as jnp
import numpy as np
from jax import lax
from jax.sharding import Mesh, PartitionSpec as P

F32 = jnp.float32
BF16 = jnp.bfloat16
GROUPED = ("dp", "x", "out", "dep")
NEIGHBOURS = ((0, 1), (1, 0), (2, 3), (3, 2))


def plane_groups(micro, chips, line, quarters):
    place = np.arange(micro * chips * line * quarters).reshape(micro, chips, line, quarters)
    paired = np.stack([place[m][:, :, np.arange(quarters) ^ m] for m in range(micro)], axis=1)
    return paired.reshape(-1, quarters).T.tolist()


def per_device(tokens, gate_weight, up_weight, cotangent):
    rows, feature = tokens.shape[1], tokens.shape[2]
    units = gate_weight.shape[1]
    quarters = lax.axis_size("dep")
    micro = lax.axis_size("dp")
    chips, line = lax.axis_size("x"), lax.axis_size("out")
    lanes = line * rows
    peers = chips * micro * line
    groups = plane_groups(micro, chips, line, quarters)
    first = lax.axis_index("core") == 0
    group = lax.axis_index("dp") == 0

    def swap(block):
        return lax.ppermute(block, "core", ((0, 1), (1, 0)))

    def paired(even, odd):
        return jnp.where(first, even, odd), jnp.where(first, odd, even)

    def near_first(own, far):
        return jnp.stack([jnp.where(group, own, far), jnp.where(group, far, own)])

    def exchange(blocks):
        return lax.all_to_all(blocks, GROUPED, 0, 0, axis_index_groups=groups, tiled=True)

    handed = lax.ppermute(tokens[0], "dep", NEIGHBOURS)
    sent = near_first(tokens[0], handed)[None, :, None]
    own_tokens = exchange(
        jnp.broadcast_to(sent, (chips, micro, line, rows, feature)).reshape(-1, rows, feature)
    ).reshape(-1, feature)

    weights = (gate_weight, swap(gate_weight), up_weight, swap(up_weight))
    cot = cotangent.reshape(micro, 2, lanes, units)
    cot_own, cot_sent = paired(cot[:, 0], cot[:, 1])
    cot_vals = jnp.concatenate([cot_own, swap(cot_sent)], axis=2).reshape(-1, 2 * units)
    cot_vals = cot_vals.astype(F32)

    partial = jnp.concatenate(
        [jnp.dot(own_tokens, w, preferred_element_type=F32).astype(BF16) for w in weights],
        axis=1,
    )
    received = lax.all_to_all(
        partial.reshape(quarters, -1, 4 * units), "dep", 0, 0, tiled=True
    )
    summed = jnp.sum(received.astype(F32), axis=0)
    gate_vals, up_vals = summed[:, : 2 * units], summed[:, 2 * units :]

    sig_gate = jax.nn.sigmoid(gate_vals)
    silu_gate = gate_vals * sig_gate
    hidden = (silu_gate * up_vals).astype(BF16).reshape(micro, lanes, 2 * units)
    d_gate = (cot_vals * up_vals * sig_gate * (1.0 + gate_vals * (1.0 - sig_gate))).astype(BF16)
    d_up = (cot_vals * silu_gate).astype(BF16)
    mine = jnp.concatenate([d_gate, d_up], axis=1)
    full = lax.all_to_all(
        jnp.broadcast_to(mine[None], (quarters,) + mine.shape), "dep", 0, 0, tiled=True
    ).reshape(-1, 4 * units)

    parts = [full[:, k * units : (k + 1) * units] for k in range(4)]
    across = (((1,), (1,)), ((), ()))
    chip_sum = sum(
        lax.dot_general(part, w, across, preferred_element_type=F32)
        for part, w in zip(parts, weights)
    ).astype(BF16)
    blocks = chip_sum.reshape(peers, rows, -1, 128).swapaxes(1, 2)
    pieces = exchange(blocks.reshape(peers, -1, 128))
    pieces = pieces.reshape(chips, micro, line, -1, 128).astype(F32)
    from_zero, from_one = (jnp.sum(pieces[:, m], axis=(0, 1)) for m in range(micro))
    near = jnp.where(group, from_zero, from_one)
    far = lax.ppermute(jnp.where(group, from_one, from_zero), "dep", NEIGHBOURS)
    input_grad = (near + far).astype(BF16).reshape(-1, rows, 128).swapaxes(0, 1)

    other_tokens = swap(own_tokens)
    def grad(own, sent):
        contract = (((0,), (0,)), ((), ()))
        return (
            lax.dot_general(own_tokens, own, contract, preferred_element_type=F32)
            + lax.dot_general(other_tokens, swap(sent), contract, preferred_element_type=F32)
        ).astype(BF16)

    hid = paired(hidden[:, :, :units], swap(hidden[:, :, units:]))
    return (
        jnp.stack(hid, axis=1).reshape(cotangent.shape),
        input_grad.reshape(tokens.shape),
        grad(parts[0], parts[1]),
        grad(parts[2], parts[3]),
    )


def solution(mesh):
    dp, inp, out, dep = (mesh.shape[name] for name in ("dp", "inp", "out", "dep"))
    split = Mesh(
        np.asarray(mesh.devices).reshape(dp, inp // 2, 2, out, dep),
        ("dp", "x", "core", "out", "dep"),
    )
    tokens_at = P("dp", ("x", "core", "out"), "dep")
    weight_at = P("dep", ("dp", "x", "core", "out"))
    hidden_at = P(None, "dep", ("dp", "x", "core", "out"))
    return jax.shard_map(
        per_device,
        mesh=split,
        in_specs=(tokens_at, weight_at, weight_at, hidden_at),
        out_specs=(hidden_at, tokens_at, weight_at, weight_at),
        check_vma=False,
    )
```

```python
import jax
import jax.numpy as jnp
import numpy as np
from jax import lax
from jax.experimental import pallas as pl
from jax.experimental.pallas import tpu as pltpu
from jax.sharding import Mesh, PartitionSpec as P

F32 = jnp.float32
BF16 = jnp.bfloat16
CHIPS = ("x", "dp", "out")


VMEM = pl.BlockSpec(memory_space=pltpu.VMEM)
ANYWHERE = pl.BlockSpec(memory_space=pl.ANY)
PARAMS = pltpu.CompilerParams(vmem_limit_bytes=24 * 1024 * 1024)
CHUNKS = 4


def forward_kernel(tokens, w0, w1, w2, w3, partial, held, arrived):
    units = w0.shape[1]
    copies = [
        pltpu.make_async_copy(w, held.at[k], arrived.at[k])
        for k, w in enumerate((w0, w1, w2, w3))
    ]
    for copy in copies:
        copy.start()
    for k, copy in enumerate(copies):
        copy.wait()
        block = jnp.dot(tokens[...], held[k], preferred_element_type=F32)
        partial[:, k * units : (k + 1) * units] = block.astype(BF16)


def backward_kernel(full, w0, w1, w2, w3, total, held, arrived):
    feature, units = w0.shape
    size = feature // CHUNKS
    copies = [
        [
            pltpu.make_async_copy(
                w.at[pl.ds(c * size, size)], held.at[k, pl.ds(c * size, size)], arrived.at[c, k]
            )
            for k, w in enumerate((w0, w1, w2, w3))
        ]
        for c in range(CHUNKS)
    ]
    for chunk in copies:
        for copy in chunk:
            copy.start()
    for c, chunk in enumerate(copies):
        for copy in chunk:
            copy.wait()
        total[:, c * size : (c + 1) * size] = sum(
            lax.dot_general(
                full[:, k * units : (k + 1) * units],
                held[k, c * size : (c + 1) * size],
                (((1,), (1,)), ((), ())),
                preferred_element_type=F32,
            )
            for k in range(4)
        ).astype(BF16)


def gradient_kernel(own_tokens, other_tokens, full, other_d, gate, up):
    feature, units = gate.shape
    size = feature // CHUNKS
    contract = (((0,), (0,)), ((), ()))
    for c in range(CHUNKS):
        span = slice(c * size, (c + 1) * size)
        tokens = jnp.concatenate([own_tokens[:, span], other_tokens[:, span]], axis=0).T
        for k, out in enumerate((gate, up)):
            d = jnp.concatenate(
                [
                    full[:, 2 * k * units : (2 * k + 1) * units],
                    other_d[:, k * units : (k + 1) * units],
                ],
                axis=0,
            )
            out[span] = jnp.dot(tokens, d, preferred_element_type=F32).astype(BF16)


def with_weights(kernel, name, left, weights, out_shape, sems):
    feature, units = weights[0].shape
    return pl.pallas_call(
        kernel,
        out_shape=jax.ShapeDtypeStruct(out_shape, BF16),
        in_specs=[VMEM] + [ANYWHERE] * 4,
        out_specs=VMEM,
        scratch_shapes=[
            pltpu.VMEM((4, feature, units), BF16),
            pltpu.SemaphoreType.DMA(sems),
        ],
        compiler_params=PARAMS,
        cost_estimate=pl.CostEstimate(
            flops=8 * left.shape[0] * feature * units,
            bytes_accessed=8 * feature * units,
            transcendentals=0,
        ),
        name=name,
    )(left, *weights)


def gradients(own_tokens, other_tokens, full, other_d, units):
    feature = own_tokens.shape[1]
    shape = jax.ShapeDtypeStruct((feature, units), BF16)
    return pl.pallas_call(
        gradient_kernel,
        out_shape=(shape, shape),
        in_specs=[VMEM] * 4,
        out_specs=(VMEM, VMEM),
        compiler_params=PARAMS,
        cost_estimate=pl.CostEstimate(
            flops=8 * own_tokens.shape[0] * feature * units,
            bytes_accessed=8 * feature * units,
            transcendentals=0,
        ),
        name="gradients",
    )(own_tokens, other_tokens, full, other_d)


def per_device(tokens, gate_weight, up_weight, cotangent):
    rows, feature = tokens.shape[1], tokens.shape[2]
    units = gate_weight.shape[1]
    quarters = lax.axis_size("dep")
    micro = lax.axis_size("dp")
    lanes = lax.axis_size("out") * rows
    peers = lax.axis_size("x") * micro * lax.axis_size("out")
    first = lax.axis_index("core") == 0

    def swap(block):
        return lax.ppermute(block, "core", ((0, 1), (1, 0)))

    def paired(even, odd):
        return jnp.where(first, even, odd), jnp.where(first, odd, even)

    own_tokens = lax.all_to_all(
        jnp.broadcast_to(tokens, (peers, rows, feature)), CHIPS, 0, 0, tiled=True
    ).reshape(-1, feature)

    weights = (gate_weight, swap(gate_weight), up_weight, swap(up_weight))
    cot = cotangent.reshape(micro, 2, lanes, units)
    cot_own, cot_sent = paired(cot[:, 0], cot[:, 1])
    cot_vals = jnp.concatenate([cot_own, swap(cot_sent)], axis=2).reshape(-1, 2 * units)
    cot_vals = cot_vals.astype(F32)

    count = own_tokens.shape[0]
    partial = with_weights(
        forward_kernel, "forward", own_tokens, weights, (count, 4 * units), (4,)
    )
    received = lax.all_to_all(
        partial.reshape(quarters, -1, 4 * units), "dep", 0, 0, tiled=True
    )
    summed = jnp.sum(received.astype(F32), axis=0)
    gate_vals, up_vals = summed[:, : 2 * units], summed[:, 2 * units :]

    sig_gate = jax.nn.sigmoid(gate_vals)
    silu_gate = gate_vals * sig_gate
    hidden = (silu_gate * up_vals).astype(BF16).reshape(micro, lanes, 2 * units)
    d_gate = (cot_vals * up_vals * sig_gate * (1.0 + gate_vals * (1.0 - sig_gate))).astype(BF16)
    d_up = (cot_vals * silu_gate).astype(BF16)
    mine = jnp.concatenate([d_gate, d_up], axis=1)
    full = lax.all_to_all(
        jnp.broadcast_to(mine[None], (quarters,) + mine.shape), "dep", 0, 0, tiled=True
    ).reshape(-1, 4 * units)

    chip_sum = with_weights(
        backward_kernel, "backward", full, weights, (count, feature), (CHUNKS, 4)
    )
    blocks = chip_sum.reshape(peers, rows, -1, 128).swapaxes(1, 2)
    pieces = lax.all_to_all(blocks.reshape(peers, -1, 128), CHIPS, 0, 0, tiled=True)
    input_grad = jnp.sum(pieces.astype(F32), axis=0).astype(BF16)
    input_grad = input_grad.reshape(-1, rows, 128).swapaxes(0, 1)

    other_tokens = swap(own_tokens)
    sent = jnp.concatenate([full[:, units : 2 * units], full[:, 3 * units :]], axis=1)
    gate_grad, up_grad = gradients(own_tokens, other_tokens, full, swap(sent), units)

    hid = paired(hidden[:, :, :units], swap(hidden[:, :, units:]))
    return (
        jnp.stack(hid, axis=1).reshape(cotangent.shape),
        input_grad.reshape(tokens.shape),
        gate_grad,
        up_grad,
    )


def solution(mesh):
    dp, inp, out, dep = (mesh.shape[name] for name in ("dp", "inp", "out", "dep"))
    split = Mesh(
        np.asarray(mesh.devices).reshape(dp, inp // 2, 2, out, dep),
        ("dp", "x", "core", "out", "dep"),
    )
    tokens_at = P("dp", ("x", "core", "out"), "dep")
    weight_at = P("dep", ("dp", "x", "core", "out"))
    hidden_at = P(None, "dep", ("dp", "x", "core", "out"))
    return jax.shard_map(
        per_device,
        mesh=split,
        in_specs=(tokens_at, weight_at, weight_at, hidden_at),
        out_specs=(hidden_at, tokens_at, weight_at, weight_at),
        check_vma=False,
    )
```

```python
import jax
import jax.numpy as jnp
import numpy as np
from jax import lax
from jax.experimental import pallas as pl
from jax.experimental.pallas import tpu as pltpu
from jax.sharding import Mesh, PartitionSpec as P

F32 = jnp.float32
BF16 = jnp.bfloat16
CHIPS = ("x", "dp", "out")


VMEM = pl.BlockSpec(memory_space=pltpu.VMEM)
HBM = pl.BlockSpec(memory_space=pltpu.HBM)
PARAMS = pltpu.CompilerParams(vmem_limit_bytes=24 * 1024 * 1024)
CHUNKS = 4


def forward_kernel(tokens, w0, w1, w2, w3, partial, held, arrived):
    units = w0.shape[1]
    copies = [
        pltpu.make_async_copy(w, held.at[k], arrived.at[k])
        for k, w in enumerate((w0, w1, w2, w3))
    ]
    for copy in copies:
        copy.start()
    for k, copy in enumerate(copies):
        copy.wait()
        block = jnp.dot(tokens[...], held[k], preferred_element_type=F32)
        partial[:, k * units : (k + 1) * units] = block.astype(BF16)


def backward_kernel(full, w0, w1, w2, w3, total, held, arrived):
    feature, units = w0.shape
    size = feature // CHUNKS
    copies = [
        [
            pltpu.make_async_copy(
                w.at[pl.ds(c * size, size)], held.at[k, pl.ds(c * size, size)], arrived.at[c, k]
            )
            for k, w in enumerate((w0, w1, w2, w3))
        ]
        for c in range(CHUNKS)
    ]
    for chunk in copies:
        for copy in chunk:
            copy.start()
    for c, chunk in enumerate(copies):
        for copy in chunk:
            copy.wait()
        total[:, c * size : (c + 1) * size] = sum(
            lax.dot_general(
                full[:, k * units : (k + 1) * units],
                held[k, c * size : (c + 1) * size],
                (((1,), (1,)), ((), ())),
                preferred_element_type=F32,
            )
            for k in range(4)
        ).astype(BF16)


def gradient_kernel(own_tokens, other_tokens, full, other_d, gate, up):
    feature, units = gate.shape
    size = feature // CHUNKS
    contract = (((0,), (0,)), ((), ()))
    for c in range(CHUNKS):
        span = slice(c * size, (c + 1) * size)
        tokens = jnp.concatenate([own_tokens[:, span], other_tokens[:, span]], axis=0).T
        for k, out in enumerate((gate, up)):
            d = jnp.concatenate(
                [
                    full[:, 2 * k * units : (2 * k + 1) * units],
                    other_d[:, k * units : (k + 1) * units],
                ],
                axis=0,
            )
            out[span] = jnp.dot(tokens, d, preferred_element_type=F32).astype(BF16)


def with_weights(kernel, name, left, weights, out_shape, sems):
    feature, units = weights[0].shape
    return pl.pallas_call(
        kernel,
        out_shape=jax.ShapeDtypeStruct(out_shape, BF16),
        in_specs=[VMEM] + [HBM] * 4,
        out_specs=VMEM,
        scratch_shapes=[
            pltpu.VMEM((4, feature, units), BF16),
            pltpu.SemaphoreType.DMA(sems),
        ],
        compiler_params=PARAMS,
        cost_estimate=pl.CostEstimate(
            flops=8 * left.shape[0] * feature * units,
            bytes_accessed=8 * feature * units,
            transcendentals=0,
        ),
        name=name,
    )(left, *weights)


def gradients(own_tokens, other_tokens, full, other_d, units):
    feature = own_tokens.shape[1]
    shape = jax.ShapeDtypeStruct((feature, units), BF16)
    return pl.pallas_call(
        gradient_kernel,
        out_shape=(shape, shape),
        in_specs=[VMEM] * 4,
        out_specs=(VMEM, VMEM),
        compiler_params=PARAMS,
        cost_estimate=pl.CostEstimate(
            flops=8 * own_tokens.shape[0] * feature * units,
            bytes_accessed=8 * feature * units,
            transcendentals=0,
        ),
        name="gradients",
    )(own_tokens, other_tokens, full, other_d)


def per_device(tokens, gate_weight, up_weight, cotangent):
    rows, feature = tokens.shape[1], tokens.shape[2]
    units = gate_weight.shape[1]
    quarters = lax.axis_size("dep")
    micro = lax.axis_size("dp")
    lanes = lax.axis_size("out") * rows
    peers = lax.axis_size("x") * micro * lax.axis_size("out")
    first = lax.axis_index("core") == 0

    def swap(block):
        return lax.ppermute(block, "core", ((0, 1), (1, 0)))

    def paired(even, odd):
        return jnp.where(first, even, odd), jnp.where(first, odd, even)

    copies = jnp.broadcast_to(tokens, (peers, rows, feature))
    copies, gate_weight, up_weight, cotangent = lax.optimization_barrier(
        (copies, gate_weight, up_weight, cotangent)
    )
    own_tokens = lax.all_to_all(copies, CHIPS, 0, 0, tiled=True).reshape(-1, feature)

    weights = (gate_weight, swap(gate_weight), up_weight, swap(up_weight))
    cot = cotangent.reshape(micro, 2, lanes, units)
    cot_own, cot_sent = paired(cot[:, 0], cot[:, 1])
    cot_vals = jnp.concatenate([cot_own, swap(cot_sent)], axis=2).reshape(-1, 2 * units)
    cot_vals = cot_vals.astype(F32)

    count = own_tokens.shape[0]
    partial = with_weights(
        forward_kernel, "forward", own_tokens, weights, (count, 4 * units), (4,)
    )
    received = lax.all_to_all(
        partial.reshape(quarters, -1, 4 * units), "dep", 0, 0, tiled=True
    )
    summed = jnp.sum(received.astype(F32), axis=0)
    gate_vals, up_vals = summed[:, : 2 * units], summed[:, 2 * units :]

    sig_gate = jax.nn.sigmoid(gate_vals)
    silu_gate = gate_vals * sig_gate
    hidden = (silu_gate * up_vals).astype(BF16).reshape(micro, lanes, 2 * units)
    d_gate = (cot_vals * up_vals * sig_gate * (1.0 + gate_vals * (1.0 - sig_gate))).astype(BF16)
    d_up = (cot_vals * silu_gate).astype(BF16)
    mine = jnp.concatenate([d_gate, d_up], axis=1)
    full = lax.all_to_all(
        jnp.broadcast_to(mine[None], (quarters,) + mine.shape), "dep", 0, 0, tiled=True
    ).reshape(-1, 4 * units)

    chip_sum = with_weights(
        backward_kernel, "backward", full, weights, (count, feature), (CHUNKS, 4)
    )
    blocks = chip_sum.reshape(peers, rows, -1, 128).swapaxes(1, 2)
    pieces = lax.all_to_all(blocks.reshape(peers, -1, 128), CHIPS, 0, 0, tiled=True)
    input_grad = jnp.sum(pieces.astype(F32), axis=0).astype(BF16)
    input_grad = input_grad.reshape(-1, rows, 128).swapaxes(0, 1)

    other_tokens = swap(own_tokens)
    sent = jnp.concatenate([full[:, units : 2 * units], full[:, 3 * units :]], axis=1)
    gate_grad, up_grad = gradients(own_tokens, other_tokens, full, swap(sent), units)

    hid = paired(hidden[:, :, :units], swap(hidden[:, :, units:]))
    return (
        jnp.stack(hid, axis=1).reshape(cotangent.shape),
        input_grad.reshape(tokens.shape),
        gate_grad,
        up_grad,
    )


def solution(mesh):
    dp, inp, out, dep = (mesh.shape[name] for name in ("dp", "inp", "out", "dep"))
    split = Mesh(
        np.asarray(mesh.devices).reshape(dp, inp // 2, 2, out, dep),
        ("dp", "x", "core", "out", "dep"),
    )
    tokens_at = P("dp", ("x", "core", "out"), "dep")
    weight_at = P("dep", ("dp", "x", "core", "out"))
    hidden_at = P(None, "dep", ("dp", "x", "core", "out"))
    return jax.shard_map(
        per_device,
        mesh=split,
        in_specs=(tokens_at, weight_at, weight_at, hidden_at),
        out_specs=(hidden_at, tokens_at, weight_at, weight_at),
        check_vma=False,
    )
```

```python
import jax
import jax.numpy as jnp
import numpy as np
from jax import lax
from jax.experimental import pallas as pl
from jax.experimental.pallas import tpu as pltpu
from jax.sharding import Mesh, PartitionSpec as P

F32 = jnp.float32
BF16 = jnp.bfloat16
CHIPS = ("x", "dp", "out")


VMEM = pl.BlockSpec(memory_space=pltpu.VMEM)
HBM = pl.BlockSpec(memory_space=pltpu.HBM)
PARAMS = pltpu.CompilerParams(vmem_limit_bytes=24 * 1024 * 1024)
CHUNKS = 4


def copies_kernel(tokens, copies):
    copies[...] = jnp.broadcast_to(tokens[...], copies.shape)


def own_kernel(pieces, w0, w1, flat, partial, landed, held, arrived):
    units = w0.shape[1]
    fetched = pltpu.make_async_copy(pieces, landed, arrived.at[2])
    copies = [
        pltpu.make_async_copy(w, held.at[k], arrived.at[k]) for k, w in enumerate((w0, w1))
    ]
    fetched.start()
    for copy in copies:
        copy.start()
    fetched.wait()
    flat[...] = landed[...].reshape(flat.shape)
    for k, copy in enumerate(copies):
        copy.wait()
        block = jnp.dot(flat[...], held[k], preferred_element_type=F32)
        partial[:, k * units : (k + 1) * units] = block.astype(BF16)


def other_kernel(flat, own, w0, w1, partial, held, arrived):
    units = w0.shape[1]
    copies = [
        pltpu.make_async_copy(w, held.at[k], arrived.at[k]) for k, w in enumerate((w0, w1))
    ]
    for copy in copies:
        copy.start()
    partial[:, : 2 * units] = own[...]
    for k, copy in enumerate(copies):
        copy.wait()
        block = jnp.dot(flat[...], held[k], preferred_element_type=F32)
        partial[:, (2 + k) * units : (3 + k) * units] = block.astype(BF16)


def hidden_kernel(received, cotangent, hidden, spread):
    units = cotangent.shape[1] // 2
    for h in range(2):
        at = slice(h * units, (h + 1) * units)
        gate_at = slice(2 * h * units, (2 * h + 1) * units)
        up_at = slice((2 * h + 1) * units, (2 * h + 2) * units)
        gate_vals = jnp.sum(received[:, :, gate_at].astype(F32), axis=0)
        up_vals = jnp.sum(received[:, :, up_at].astype(F32), axis=0)
        cot_vals = cotangent[:, at].astype(F32)
        sig_gate = jax.nn.sigmoid(gate_vals)
        silu_gate = gate_vals * sig_gate
        hidden[:, at] = (silu_gate * up_vals).astype(BF16)
        d_gate = cot_vals * up_vals * sig_gate * (1.0 + gate_vals * (1.0 - sig_gate))
        d_up = cot_vals * silu_gate
        for q in range(spread.shape[0]):
            spread[q, :, gate_at] = d_gate.astype(BF16)
            spread[q, :, up_at] = d_up.astype(BF16)


def backward_kernel(full, w0, w1, w2, w3, blocks, held, arrived):
    peers = blocks.shape[0]
    rows = full.shape[0] // peers
    feature, units = w0.shape
    size = feature // CHUNKS
    copies = [
        [
            pltpu.make_async_copy(
                w.at[pl.ds(c * size, size)], held.at[k, pl.ds(c * size, size)], arrived.at[c, k]
            )
            for k, w in enumerate((w0, w1, w2, w3))
        ]
        for c in range(CHUNKS)
    ]
    for chunk in copies:
        for copy in chunk:
            copy.start()
    for c, chunk in enumerate(copies):
        for copy in chunk:
            copy.wait()
        total = sum(
            lax.dot_general(
                full[:, k * units : (k + 1) * units],
                held[k, c * size : (c + 1) * size],
                (((1,), (1,)), ((), ())),
                preferred_element_type=F32,
            )
            for k in range(4)
        )
        for j in range(size // 128):
            at = (c * size // 128 + j) * rows
            tile = total[:, j * 128 : (j + 1) * 128].reshape(peers, rows, 128)
            blocks[:, at : at + rows, :] = tile.astype(BF16)


def gradient_kernel(own_tokens, other_tokens, full, other_d, gate, up):
    feature, units = gate.shape
    size = feature // CHUNKS
    contract = (((0,), (0,)), ((), ()))
    for c in range(CHUNKS):
        span = slice(c * size, (c + 1) * size)
        tokens = jnp.concatenate([own_tokens[:, span], other_tokens[:, span]], axis=0).T
        for k, out in enumerate((gate, up)):
            d = jnp.concatenate(
                [
                    full[:, k * units : (k + 1) * units],
                    other_d[:, k * units : (k + 1) * units],
                ],
                axis=0,
            )
            out[span] = jnp.dot(tokens, d, preferred_element_type=F32).astype(BF16)


def cost(rows, feature, columns):
    return pl.CostEstimate(
        flops=2 * rows * feature * columns,
        bytes_accessed=2 * feature * columns,
        transcendentals=0,
    )


def token_copies(tokens, peers):
    return pl.pallas_call(
        copies_kernel,
        out_shape=jax.ShapeDtypeStruct((peers,) + tokens.shape[1:], BF16),
        in_specs=[VMEM],
        out_specs=VMEM,
        compiler_params=PARAMS,
        name="copies",
    )(tokens)


def own_products(pieces, weights):
    peers, rows, feature = pieces.shape
    count, units = peers * rows, weights[0].shape[1]
    return pl.pallas_call(
        own_kernel,
        out_shape=(
            jax.ShapeDtypeStruct((count, feature), BF16),
            jax.ShapeDtypeStruct((count, 2 * units), BF16),
        ),
        in_specs=[HBM] * 3,
        out_specs=(VMEM, VMEM),
        scratch_shapes=[
            pltpu.VMEM(pieces.shape, BF16),
            pltpu.VMEM((2, feature, units), BF16),
            pltpu.SemaphoreType.DMA((3,)),
        ],
        compiler_params=PARAMS,
        cost_estimate=cost(8 * count, feature, 2 * units),
        name="own_products",
    )(pieces, *weights)


def other_products(flat, own, weights):
    count, feature = flat.shape
    units = weights[0].shape[1]
    return pl.pallas_call(
        other_kernel,
        out_shape=jax.ShapeDtypeStruct((count, 4 * units), BF16),
        in_specs=[VMEM] * 2 + [HBM] * 2,
        out_specs=VMEM,
        scratch_shapes=[
            pltpu.VMEM((2, feature, units), BF16),
            pltpu.SemaphoreType.DMA((2,)),
        ],
        compiler_params=PARAMS,
        cost_estimate=cost(count, feature, 2 * units),
        name="other_products",
    )(flat, own, *weights)


def hidden_and_gradients(received, cotangent):
    return pl.pallas_call(
        hidden_kernel,
        out_shape=(
            jax.ShapeDtypeStruct(cotangent.shape, BF16),
            jax.ShapeDtypeStruct(received.shape, BF16),
        ),
        in_specs=[VMEM] * 2,
        out_specs=(VMEM, VMEM),
        compiler_params=PARAMS,
        name="hidden_and_gradients",
    )(received, cotangent)


def input_blocks(full, weights, peers):
    count = full.shape[0]
    feature, units = weights[0].shape
    return pl.pallas_call(
        backward_kernel,
        out_shape=jax.ShapeDtypeStruct((peers, count * feature // peers // 128, 128), BF16),
        in_specs=[VMEM] + [HBM] * 4,
        out_specs=VMEM,
        scratch_shapes=[
            pltpu.VMEM((4, feature, units), BF16),
            pltpu.SemaphoreType.DMA((CHUNKS, 4)),
        ],
        compiler_params=PARAMS,
        cost_estimate=cost(count, feature, 4 * units),
        name="input_blocks",
    )(full, *weights)


def gradients(own_tokens, other_tokens, full, other_d, units):
    feature = own_tokens.shape[1]
    shape = jax.ShapeDtypeStruct((feature, units), BF16)
    return pl.pallas_call(
        gradient_kernel,
        out_shape=(shape, shape),
        in_specs=[VMEM] * 4,
        out_specs=(VMEM, VMEM),
        compiler_params=PARAMS,
        cost_estimate=cost(own_tokens.shape[0], feature, 4 * units),
        name="gradients",
    )(own_tokens, other_tokens, full, other_d)


def per_device(tokens, gate_weight, up_weight, cotangent):
    rows, feature = tokens.shape[1], tokens.shape[2]
    units = gate_weight.shape[1]
    quarters = lax.axis_size("dep")
    micro = lax.axis_size("dp")
    lanes = lax.axis_size("out") * rows
    peers = lax.axis_size("x") * micro * lax.axis_size("out")
    first = lax.axis_index("core") == 0

    def swap(block):
        return lax.ppermute(block, "core", ((0, 1), (1, 0)))

    def paired(even, odd):
        return jnp.where(first, even, odd), jnp.where(first, odd, even)

    arrived = lax.all_to_all(token_copies(tokens, peers), CHIPS, 0, 0, tiled=True)

    own_weights = (gate_weight, up_weight)
    other_weights = (swap(gate_weight), swap(up_weight))
    own_tokens, own_partial = own_products(arrived, own_weights)
    partial = other_products(own_tokens, own_partial, other_weights)

    cot = cotangent.reshape(micro, 2, lanes, units)
    cot_own, cot_sent = paired(cot[:, 0], cot[:, 1])
    cot = jnp.concatenate([cot_own, swap(cot_sent)], axis=2).reshape(-1, 2 * units)

    received = lax.all_to_all(
        partial.reshape(quarters, -1, 4 * units), "dep", 0, 0, tiled=True
    )
    hidden, d_copies = hidden_and_gradients(received, cot)
    hidden = hidden.reshape(micro, lanes, 2 * units)
    full = lax.all_to_all(d_copies, "dep", 0, 0, tiled=True).reshape(-1, 4 * units)

    blocks = input_blocks(full, own_weights + other_weights, peers)
    pieces = lax.all_to_all(blocks, CHIPS, 0, 0, tiled=True)
    input_grad = jnp.sum(pieces.astype(F32), axis=0).astype(BF16)
    input_grad = input_grad.reshape(-1, rows, 128).swapaxes(0, 1)

    other_tokens = swap(own_tokens)
    other_d = swap(full[:, 2 * units :])
    gate_grad, up_grad = gradients(own_tokens, other_tokens, full, other_d, units)

    hid = paired(hidden[:, :, :units], swap(hidden[:, :, units:]))
    return (
        jnp.stack(hid, axis=1).reshape(cotangent.shape),
        input_grad.reshape(tokens.shape),
        gate_grad,
        up_grad,
    )


def solution(mesh):
    dp, inp, out, dep = (mesh.shape[name] for name in ("dp", "inp", "out", "dep"))
    split = Mesh(
        np.asarray(mesh.devices).reshape(dp, inp // 2, 2, out, dep),
        ("dp", "x", "core", "out", "dep"),
    )
    tokens_at = P("dp", ("x", "core", "out"), "dep")
    weight_at = P("dep", ("dp", "x", "core", "out"))
    hidden_at = P(None, "dep", ("dp", "x", "core", "out"))
    return jax.shard_map(
        per_device,
        mesh=split,
        in_specs=(tokens_at, weight_at, weight_at, hidden_at),
        out_specs=(hidden_at, tokens_at, weight_at, weight_at),
        check_vma=False,
    )
```

```python
import jax
import jax.numpy as jnp
import numpy as np
from jax import lax
from jax.experimental import pallas as pl
from jax.experimental.pallas import tpu as pltpu
from jax.sharding import Mesh, PartitionSpec as P

F32 = jnp.float32
BF16 = jnp.bfloat16
CHIPS = ("x", "dp", "out")


VMEM = pl.BlockSpec(memory_space=pltpu.VMEM)
HBM = pl.BlockSpec(memory_space=pltpu.HBM)
MIB = 1024 * 1024
PARAMS = pltpu.CompilerParams(vmem_limit_bytes=24 * MIB)
FORWARD = pltpu.CompilerParams(vmem_limit_bytes=51 * MIB + MIB // 2)
BACKWARD = pltpu.CompilerParams(vmem_limit_bytes=49 * MIB + MIB // 2)
CHUNKS = 4


def copies_kernel(tokens, copies):
    copies[...] = jnp.broadcast_to(tokens[...], copies.shape)


def own_kernel(pieces, w0, w1, flat, partial, landed, held, arrived):
    units = w0.shape[1]
    fetched = pltpu.make_async_copy(pieces, landed, arrived.at[2])
    copies = [
        pltpu.make_async_copy(w, held.at[k], arrived.at[k]) for k, w in enumerate((w0, w1))
    ]
    fetched.start()
    for copy in copies:
        copy.start()
    fetched.wait()
    flat[...] = landed[...].reshape(flat.shape)
    for k, copy in enumerate(copies):
        copy.wait()
        block = jnp.dot(flat[...], held[k], preferred_element_type=F32)
        partial[:, k * units : (k + 1) * units] = block.astype(BF16)


def other_kernel(flat, own, w0, w1, partial, held, arrived):
    units = w0.shape[1]
    copies = [
        pltpu.make_async_copy(w, held.at[k], arrived.at[k]) for k, w in enumerate((w0, w1))
    ]
    for copy in copies:
        copy.start()
    partial[:, : 2 * units] = own[...]
    for k, copy in enumerate(copies):
        copy.wait()
        block = jnp.dot(flat[...], held[k], preferred_element_type=F32)
        partial[:, (2 + k) * units : (3 + k) * units] = block.astype(BF16)


def hidden_kernel(received, cotangent, hidden, spread):
    units = cotangent.shape[1] // 2
    for h in range(2):
        at = slice(h * units, (h + 1) * units)
        gate_at = slice(2 * h * units, (2 * h + 1) * units)
        up_at = slice((2 * h + 1) * units, (2 * h + 2) * units)
        gate_vals = jnp.sum(received[:, :, gate_at].astype(F32), axis=0)
        up_vals = jnp.sum(received[:, :, up_at].astype(F32), axis=0)
        cot_vals = cotangent[:, at].astype(F32)
        sig_gate = jax.nn.sigmoid(gate_vals)
        silu_gate = gate_vals * sig_gate
        hidden[:, at] = (silu_gate * up_vals).astype(BF16)
        d_gate = cot_vals * up_vals * sig_gate * (1.0 + gate_vals * (1.0 - sig_gate))
        d_up = cot_vals * silu_gate
        for q in range(spread.shape[0]):
            spread[q, :, gate_at] = d_gate.astype(BF16)
            spread[q, :, up_at] = d_up.astype(BF16)


def backward_kernel(full, w0, w1, w2, w3, blocks, held, arrived):
    peers = blocks.shape[0]
    rows = full.shape[0] // peers
    feature, units = w0.shape
    size = feature // CHUNKS
    copies = [
        [
            pltpu.make_async_copy(
                w.at[pl.ds(c * size, size)], held.at[k, pl.ds(c * size, size)], arrived.at[c, k]
            )
            for k, w in enumerate((w0, w1, w2, w3))
        ]
        for c in range(CHUNKS)
    ]
    for chunk in copies:
        for copy in chunk:
            copy.start()
    for c, chunk in enumerate(copies):
        for copy in chunk:
            copy.wait()
        total = sum(
            lax.dot_general(
                full[:, k * units : (k + 1) * units],
                held[k, c * size : (c + 1) * size],
                (((1,), (1,)), ((), ())),
                preferred_element_type=F32,
            )
            for k in range(4)
        )
        for j in range(size // 128):
            at = (c * size // 128 + j) * rows
            tile = total[:, j * 128 : (j + 1) * 128].reshape(peers, rows, 128)
            blocks[:, at : at + rows, :] = tile.astype(BF16)


def gradient_kernel(own_tokens, other_tokens, full, other_d, gate, up):
    feature, units = gate.shape
    size = feature // CHUNKS
    contract = (((0,), (0,)), ((), ()))
    for c in range(CHUNKS):
        span = slice(c * size, (c + 1) * size)
        tokens = jnp.concatenate([own_tokens[:, span], other_tokens[:, span]], axis=0).T
        for k, out in enumerate((gate, up)):
            d = jnp.concatenate(
                [
                    full[:, k * units : (k + 1) * units],
                    other_d[:, k * units : (k + 1) * units],
                ],
                axis=0,
            )
            out[span] = jnp.dot(tokens, d, preferred_element_type=F32).astype(BF16)


def cost(rows, feature, columns):
    return pl.CostEstimate(
        flops=2 * rows * feature * columns,
        bytes_accessed=2 * feature * columns,
        transcendentals=0,
    )


def token_copies(tokens, peers):
    return pl.pallas_call(
        copies_kernel,
        out_shape=jax.ShapeDtypeStruct((peers,) + tokens.shape[1:], BF16),
        in_specs=[VMEM],
        out_specs=VMEM,
        compiler_params=PARAMS,
        name="copies",
    )(tokens)


def own_products(pieces, weights):
    peers, rows, feature = pieces.shape
    count, units = peers * rows, weights[0].shape[1]
    return pl.pallas_call(
        own_kernel,
        out_shape=(
            jax.ShapeDtypeStruct((count, feature), BF16),
            jax.ShapeDtypeStruct((count, 2 * units), BF16),
        ),
        in_specs=[HBM] * 3,
        out_specs=(VMEM, VMEM),
        scratch_shapes=[
            pltpu.VMEM(pieces.shape, BF16),
            pltpu.VMEM((2, feature, units), BF16),
            pltpu.SemaphoreType.DMA((3,)),
        ],
        compiler_params=FORWARD,
        cost_estimate=cost(8 * count, feature, 2 * units),
        name="own_products",
    )(pieces, *weights)


def other_products(flat, own, weights):
    count, feature = flat.shape
    units = weights[0].shape[1]
    return pl.pallas_call(
        other_kernel,
        out_shape=jax.ShapeDtypeStruct((count, 4 * units), BF16),
        in_specs=[VMEM] * 2 + [HBM] * 2,
        out_specs=VMEM,
        scratch_shapes=[
            pltpu.VMEM((2, feature, units), BF16),
            pltpu.SemaphoreType.DMA((2,)),
        ],
        compiler_params=PARAMS,
        cost_estimate=cost(count, feature, 2 * units),
        name="other_products",
    )(flat, own, *weights)


def hidden_and_gradients(received, cotangent):
    return pl.pallas_call(
        hidden_kernel,
        out_shape=(
            jax.ShapeDtypeStruct(cotangent.shape, BF16),
            jax.ShapeDtypeStruct(received.shape, BF16),
        ),
        in_specs=[VMEM] * 2,
        out_specs=(VMEM, VMEM),
        compiler_params=PARAMS,
        name="hidden_and_gradients",
    )(received, cotangent)


def input_blocks(full, weights, peers):
    count = full.shape[0]
    feature, units = weights[0].shape
    return pl.pallas_call(
        backward_kernel,
        out_shape=jax.ShapeDtypeStruct((peers, count * feature // peers // 128, 128), BF16),
        in_specs=[VMEM] + [HBM] * 4,
        out_specs=VMEM,
        scratch_shapes=[
            pltpu.VMEM((4, feature, units), BF16),
            pltpu.SemaphoreType.DMA((CHUNKS, 4)),
        ],
        compiler_params=BACKWARD,
        cost_estimate=cost(count, feature, 4 * units),
        name="input_blocks",
    )(full, *weights)


def gradients(own_tokens, other_tokens, full, other_d, units):
    feature = own_tokens.shape[1]
    shape = jax.ShapeDtypeStruct((feature, units), BF16)
    return pl.pallas_call(
        gradient_kernel,
        out_shape=(shape, shape),
        in_specs=[VMEM] * 4,
        out_specs=(VMEM, VMEM),
        compiler_params=PARAMS,
        cost_estimate=cost(own_tokens.shape[0], feature, 4 * units),
        name="gradients",
    )(own_tokens, other_tokens, full, other_d)


def per_device(tokens, gate_weight, up_weight, cotangent):
    rows, feature = tokens.shape[1], tokens.shape[2]
    units = gate_weight.shape[1]
    quarters = lax.axis_size("dep")
    micro = lax.axis_size("dp")
    lanes = lax.axis_size("out") * rows
    peers = lax.axis_size("x") * micro * lax.axis_size("out")
    first = lax.axis_index("core") == 0

    def swap(block):
        return lax.ppermute(block, "core", ((0, 1), (1, 0)))

    def paired(even, odd):
        return jnp.where(first, even, odd), jnp.where(first, odd, even)

    arrived = lax.all_to_all(token_copies(tokens, peers), CHIPS, 0, 0, tiled=True)

    own_weights = (gate_weight, up_weight)
    other_weights = (swap(gate_weight), swap(up_weight))
    own_tokens, own_partial = own_products(arrived, own_weights)
    partial = other_products(own_tokens, own_partial, other_weights)

    cot = cotangent.reshape(micro, 2, lanes, units)
    cot_own, cot_sent = paired(cot[:, 0], cot[:, 1])
    cot = jnp.concatenate([cot_own, swap(cot_sent)], axis=2).reshape(-1, 2 * units)

    received = lax.all_to_all(
        partial.reshape(quarters, -1, 4 * units), "dep", 0, 0, tiled=True
    )
    hidden, d_copies = hidden_and_gradients(received, cot)
    hidden = hidden.reshape(micro, lanes, 2 * units)
    full = lax.all_to_all(d_copies, "dep", 0, 0, tiled=True).reshape(-1, 4 * units)

    blocks = input_blocks(full, own_weights + other_weights, peers)
    pieces = lax.all_to_all(blocks, CHIPS, 0, 0, tiled=True)
    input_grad = jnp.sum(pieces.astype(F32), axis=0).astype(BF16)
    input_grad = input_grad.reshape(-1, rows, 128).swapaxes(0, 1)

    other_tokens = swap(own_tokens)
    other_d = swap(full[:, 2 * units :])
    gate_grad, up_grad = gradients(own_tokens, other_tokens, full, other_d, units)

    hid = paired(hidden[:, :, :units], swap(hidden[:, :, units:]))
    return (
        jnp.stack(hid, axis=1).reshape(cotangent.shape),
        input_grad.reshape(tokens.shape),
        gate_grad,
        up_grad,
    )


def solution(mesh):
    dp, inp, out, dep = (mesh.shape[name] for name in ("dp", "inp", "out", "dep"))
    split = Mesh(
        np.asarray(mesh.devices).reshape(dp, inp // 2, 2, out, dep),
        ("dp", "x", "core", "out", "dep"),
    )
    tokens_at = P("dp", ("x", "core", "out"), "dep")
    weight_at = P("dep", ("dp", "x", "core", "out"))
    hidden_at = P(None, "dep", ("dp", "x", "core", "out"))
    return jax.shard_map(
        per_device,
        mesh=split,
        in_specs=(tokens_at, weight_at, weight_at, hidden_at),
        out_specs=(hidden_at, tokens_at, weight_at, weight_at),
        check_vma=False,
    )
```

```python
import jax
import jax.numpy as jnp
import numpy as np
from jax import lax
from jax.experimental import pallas as pl
from jax.experimental.pallas import tpu as pltpu
from jax.sharding import Mesh, PartitionSpec as P

F32 = jnp.float32
BF16 = jnp.bfloat16
CHIPS = ("x", "dp", "out")


VMEM = pl.BlockSpec(memory_space=pltpu.VMEM)
HBM = pl.BlockSpec(memory_space=pltpu.HBM)
MIB = 1024 * 1024
PARAMS = pltpu.CompilerParams(vmem_limit_bytes=24 * MIB)
FORWARD = pltpu.CompilerParams(vmem_limit_bytes=51 * MIB + MIB // 2)
BACKWARD = pltpu.CompilerParams(vmem_limit_bytes=49 * MIB + MIB // 2)
CHUNKS = 2
GRAD_CHUNKS = 4


def copies_kernel(tokens, copies):
    copies[...] = jnp.broadcast_to(tokens[...], copies.shape)


def own_kernel(pieces, w0, w1, flat, partial, landed, held, arrived):
    units = w0.shape[1]
    fetched = pltpu.make_async_copy(pieces, landed, arrived.at[2])
    copies = [
        pltpu.make_async_copy(w, held.at[k], arrived.at[k]) for k, w in enumerate((w0, w1))
    ]
    fetched.start()
    copies[0].start()
    fetched.wait()
    copies[1].start()
    flat[...] = landed[...].reshape(flat.shape)
    for k, copy in enumerate(copies):
        copy.wait()
        block = jnp.dot(flat[...], held[k], preferred_element_type=F32)
        partial[:, k * units : (k + 1) * units] = block.astype(BF16)


def other_kernel(flat, own, w0, w1, partial, held, arrived):
    units = w0.shape[1]
    copies = [
        pltpu.make_async_copy(w, held.at[k], arrived.at[k]) for k, w in enumerate((w0, w1))
    ]
    for copy in copies:
        copy.start()
    partial[:, : 2 * units] = own[...]
    for k, copy in enumerate(copies):
        copy.wait()
        block = jnp.dot(flat[...], held[k], preferred_element_type=F32)
        partial[:, (2 + k) * units : (3 + k) * units] = block.astype(BF16)


def hidden_kernel(received, cotangent, hidden, spread):
    units = cotangent.shape[1] // 2
    for h in range(2):
        at = slice(h * units, (h + 1) * units)
        gate_at = slice(2 * h * units, (2 * h + 1) * units)
        up_at = slice((2 * h + 1) * units, (2 * h + 2) * units)
        gate_vals = jnp.sum(received[:, :, gate_at].astype(F32), axis=0)
        up_vals = jnp.sum(received[:, :, up_at].astype(F32), axis=0)
        cot_vals = cotangent[:, at].astype(F32)
        sig_gate = jax.nn.sigmoid(gate_vals)
        silu_gate = gate_vals * sig_gate
        hidden[:, at] = (silu_gate * up_vals).astype(BF16)
        d_gate = cot_vals * up_vals * sig_gate * (1.0 + gate_vals * (1.0 - sig_gate))
        d_up = cot_vals * silu_gate
        for q in range(spread.shape[0]):
            spread[q, :, gate_at] = d_gate.astype(BF16)
            spread[q, :, up_at] = d_up.astype(BF16)


def backward_kernel(full, w0, w1, w2, w3, blocks, held, arrived):
    peers = blocks.shape[0]
    rows = full.shape[0] // peers
    feature, units = w0.shape
    size = feature // CHUNKS
    copies = [
        [
            pltpu.make_async_copy(
                w.at[pl.ds(c * size, size)], held.at[k, pl.ds(c * size, size)], arrived.at[c, k]
            )
            for k, w in enumerate((w0, w1, w2, w3))
        ]
        for c in range(CHUNKS)
    ]
    for copy in copies[0]:
        copy.start()
    for c, chunk in enumerate(copies):
        for copy in chunk:
            copy.wait()
        if c + 1 < CHUNKS:
            for copy in copies[c + 1]:
                copy.start()
        total = sum(
            lax.dot_general(
                full[:, k * units : (k + 1) * units],
                held[k, c * size : (c + 1) * size],
                (((1,), (1,)), ((), ())),
                preferred_element_type=F32,
            )
            for k in range(4)
        )
        for j in range(size // 128):
            at = (c * size // 128 + j) * rows
            tile = total[:, j * 128 : (j + 1) * 128].astype(BF16)
            blocks[:, at : at + rows, :] = tile.reshape(peers, rows, 128)


def gradient_kernel(own_tokens, other_tokens, full, other_d, gate, up):
    feature, units = gate.shape
    size = feature // GRAD_CHUNKS
    contract = (((0,), (0,)), ((), ()))
    for c in range(GRAD_CHUNKS):
        span = slice(c * size, (c + 1) * size)
        tokens = jnp.concatenate([own_tokens[:, span], other_tokens[:, span]], axis=0).T
        for k, out in enumerate((gate, up)):
            d = jnp.concatenate(
                [
                    full[:, k * units : (k + 1) * units],
                    other_d[:, k * units : (k + 1) * units],
                ],
                axis=0,
            )
            out[span] = jnp.dot(tokens, d, preferred_element_type=F32).astype(BF16)


def cost(rows, feature, columns):
    return pl.CostEstimate(
        flops=2 * rows * feature * columns,
        bytes_accessed=2 * feature * columns,
        transcendentals=0,
    )


def token_copies(tokens, peers):
    return pl.pallas_call(
        copies_kernel,
        out_shape=jax.ShapeDtypeStruct((peers,) + tokens.shape[1:], BF16),
        in_specs=[VMEM],
        out_specs=VMEM,
        compiler_params=PARAMS,
        name="copies",
    )(tokens)


def own_products(pieces, weights):
    peers, rows, feature = pieces.shape
    count, units = peers * rows, weights[0].shape[1]
    return pl.pallas_call(
        own_kernel,
        out_shape=(
            jax.ShapeDtypeStruct((count, feature), BF16),
            jax.ShapeDtypeStruct((count, 2 * units), BF16),
        ),
        in_specs=[HBM] * 3,
        out_specs=(VMEM, VMEM),
        scratch_shapes=[
            pltpu.VMEM(pieces.shape, BF16),
            pltpu.VMEM((2, feature, units), BF16),
            pltpu.SemaphoreType.DMA((3,)),
        ],
        compiler_params=FORWARD,
        cost_estimate=cost(8 * count, feature, 2 * units),
        name="own_products",
    )(pieces, *weights)


def other_products(flat, own, weights):
    count, feature = flat.shape
    units = weights[0].shape[1]
    return pl.pallas_call(
        other_kernel,
        out_shape=jax.ShapeDtypeStruct((count, 4 * units), BF16),
        in_specs=[VMEM] * 2 + [HBM] * 2,
        out_specs=VMEM,
        scratch_shapes=[
            pltpu.VMEM((2, feature, units), BF16),
            pltpu.SemaphoreType.DMA((2,)),
        ],
        compiler_params=PARAMS,
        cost_estimate=cost(count, feature, 2 * units),
        name="other_products",
    )(flat, own, *weights)


def hidden_and_gradients(received, cotangent):
    return pl.pallas_call(
        hidden_kernel,
        out_shape=(
            jax.ShapeDtypeStruct(cotangent.shape, BF16),
            jax.ShapeDtypeStruct(received.shape, BF16),
        ),
        in_specs=[VMEM] * 2,
        out_specs=(VMEM, VMEM),
        compiler_params=PARAMS,
        name="hidden_and_gradients",
    )(received, cotangent)


def input_blocks(full, weights, peers):
    count = full.shape[0]
    feature, units = weights[0].shape
    return pl.pallas_call(
        backward_kernel,
        out_shape=jax.ShapeDtypeStruct((peers, count * feature // peers // 128, 128), BF16),
        in_specs=[VMEM] + [HBM] * 4,
        out_specs=VMEM,
        scratch_shapes=[
            pltpu.VMEM((4, feature, units), BF16),
            pltpu.SemaphoreType.DMA((CHUNKS, 4)),
        ],
        compiler_params=BACKWARD,
        cost_estimate=cost(count, feature, 4 * units),
        name="input_blocks",
    )(full, *weights)


def gradients(own_tokens, other_tokens, full, other_d, units):
    feature = own_tokens.shape[1]
    shape = jax.ShapeDtypeStruct((feature, units), BF16)
    return pl.pallas_call(
        gradient_kernel,
        out_shape=(shape, shape),
        in_specs=[VMEM] * 4,
        out_specs=(VMEM, VMEM),
        compiler_params=PARAMS,
        cost_estimate=cost(own_tokens.shape[0], feature, 4 * units),
        name="gradients",
    )(own_tokens, other_tokens, full, other_d)


def per_device(tokens, gate_weight, up_weight, cotangent):
    rows, feature = tokens.shape[1], tokens.shape[2]
    units = gate_weight.shape[1]
    quarters = lax.axis_size("dep")
    micro = lax.axis_size("dp")
    lanes = lax.axis_size("out") * rows
    peers = lax.axis_size("x") * micro * lax.axis_size("out")
    first = lax.axis_index("core") == 0

    def swap(block):
        return lax.ppermute(block, "core", ((0, 1), (1, 0)))

    def paired(even, odd):
        return jnp.where(first, even, odd), jnp.where(first, odd, even)

    arrived = lax.all_to_all(token_copies(tokens, peers), CHIPS, 0, 0, tiled=True)

    own_weights = (gate_weight, up_weight)
    other_weights = (swap(gate_weight), swap(up_weight))
    own_tokens, own_partial = own_products(arrived, own_weights)
    partial = other_products(own_tokens, own_partial, other_weights)

    cot = cotangent.reshape(micro, 2, lanes, units)
    cot_own, cot_sent = paired(cot[:, 0], cot[:, 1])
    cot = jnp.concatenate([cot_own, swap(cot_sent)], axis=2).reshape(-1, 2 * units)

    received = lax.all_to_all(
        partial.reshape(quarters, -1, 4 * units), "dep", 0, 0, tiled=True
    )
    hidden, d_copies = hidden_and_gradients(received, cot)
    hidden = hidden.reshape(micro, lanes, 2 * units)
    full = lax.all_to_all(d_copies, "dep", 0, 0, tiled=True).reshape(-1, 4 * units)

    blocks = input_blocks(full, own_weights + other_weights, peers)
    pieces = lax.all_to_all(blocks, CHIPS, 0, 0, tiled=True)
    input_grad = jnp.sum(pieces.astype(F32), axis=0).astype(BF16)
    input_grad = input_grad.reshape(-1, rows, 128).swapaxes(0, 1)

    other_tokens = swap(own_tokens)
    other_d = swap(full[:, 2 * units :])
    gate_grad, up_grad = gradients(own_tokens, other_tokens, full, other_d, units)

    hid = paired(hidden[:, :, :units], swap(hidden[:, :, units:]))
    return (
        jnp.stack(hid, axis=1).reshape(cotangent.shape),
        input_grad.reshape(tokens.shape),
        gate_grad,
        up_grad,
    )


def solution(mesh):
    dp, inp, out, dep = (mesh.shape[name] for name in ("dp", "inp", "out", "dep"))
    split = Mesh(
        np.asarray(mesh.devices).reshape(dp, inp // 2, 2, out, dep),
        ("dp", "x", "core", "out", "dep"),
    )
    tokens_at = P("dp", ("x", "core", "out"), "dep")
    weight_at = P("dep", ("dp", "x", "core", "out"))
    hidden_at = P(None, "dep", ("dp", "x", "core", "out"))
    return jax.shard_map(
        per_device,
        mesh=split,
        in_specs=(tokens_at, weight_at, weight_at, hidden_at),
        out_specs=(hidden_at, tokens_at, weight_at, weight_at),
        check_vma=False,
    )
```

```python
import jax
import jax.numpy as jnp
import numpy as np
from jax import lax
from jax.experimental import pallas as pl
from jax.experimental.pallas import tpu as pltpu
from jax.sharding import Mesh, PartitionSpec as P

F32 = jnp.float32
BF16 = jnp.bfloat16
CHIPS = ("x", "dp", "out")


VMEM = pl.BlockSpec(memory_space=pltpu.VMEM)
HBM = pl.BlockSpec(memory_space=pltpu.HBM)
MIB = 1024 * 1024
PARAMS = pltpu.CompilerParams(vmem_limit_bytes=24 * MIB)
FORWARD = pltpu.CompilerParams(vmem_limit_bytes=51 * MIB + MIB // 2)
BACKWARD = pltpu.CompilerParams(vmem_limit_bytes=52 * MIB)
CHUNKS = 2
GRAD_CHUNKS = 4


def copies_kernel(tokens, copies):
    copies[...] = jnp.broadcast_to(tokens[...], copies.shape)


def own_kernel(pieces, w0, w1, flat, partial, landed, held, arrived):
    units = w0.shape[1]
    fetched = pltpu.make_async_copy(pieces, landed, arrived.at[2])
    copies = [
        pltpu.make_async_copy(w, held.at[k], arrived.at[k]) for k, w in enumerate((w0, w1))
    ]
    fetched.start()
    for copy in copies:
        copy.start()
    fetched.wait()
    flat[...] = landed[...].reshape(flat.shape)
    for k, copy in enumerate(copies):
        copy.wait()
        block = jnp.dot(flat[...], held[k], preferred_element_type=F32)
        partial[:, k * units : (k + 1) * units] = block.astype(BF16)


def other_kernel(flat, own, w0, w1, partial, held, arrived):
    units = w0.shape[1]
    copies = [
        pltpu.make_async_copy(w, held.at[k], arrived.at[k]) for k, w in enumerate((w0, w1))
    ]
    for copy in copies:
        copy.start()
    partial[:, : 2 * units] = own[...]
    for k, copy in enumerate(copies):
        copy.wait()
        block = jnp.dot(flat[...], held[k], preferred_element_type=F32)
        partial[:, (2 + k) * units : (3 + k) * units] = block.astype(BF16)


def hidden_kernel(received, cotangent, hidden, spread):
    units = cotangent.shape[1] // 2
    for h in range(2):
        at = slice(h * units, (h + 1) * units)
        gate_at = slice(2 * h * units, (2 * h + 1) * units)
        up_at = slice((2 * h + 1) * units, (2 * h + 2) * units)
        gate_vals = jnp.sum(received[:, :, gate_at].astype(F32), axis=0)
        up_vals = jnp.sum(received[:, :, up_at].astype(F32), axis=0)
        cot_vals = cotangent[:, at].astype(F32)
        sig_gate = jax.nn.sigmoid(gate_vals)
        silu_gate = gate_vals * sig_gate
        hidden[:, at] = (silu_gate * up_vals).astype(BF16)
        d_gate = cot_vals * up_vals * sig_gate * (1.0 + gate_vals * (1.0 - sig_gate))
        d_up = cot_vals * silu_gate
        for q in range(spread.shape[0]):
            spread[q, :, gate_at] = d_gate.astype(BF16)
            spread[q, :, up_at] = d_up.astype(BF16)


def backward_kernel(full, w0, w1, w2, w3, blocks, held, arrived):
    peers = blocks.shape[0]
    rows = full.shape[0] // peers
    feature, units = w0.shape
    size = feature // CHUNKS
    copies = [
        [
            pltpu.make_async_copy(
                w.at[pl.ds(c * size, size)], held.at[k, pl.ds(c * size, size)], arrived.at[c, k]
            )
            for k, w in enumerate((w0, w1, w2, w3))
        ]
        for c in range(CHUNKS)
    ]
    for copy in copies[0]:
        copy.start()
    for c, chunk in enumerate(copies):
        for copy in chunk:
            copy.wait()
        if c + 1 < CHUNKS:
            for copy in copies[c + 1]:
                copy.start()
        total = sum(
            lax.dot_general(
                full[:, k * units : (k + 1) * units],
                held[k, c * size : (c + 1) * size],
                (((1,), (1,)), ((), ())),
                preferred_element_type=F32,
            )
            for k in range(4)
        )
        for j in range(size // 128):
            at = (c * size // 128 + j) * rows
            tile = total[:, j * 128 : (j + 1) * 128].astype(BF16)
            blocks[:, at : at + rows, :] = tile.reshape(peers, rows, 128)


def gradient_kernel(own_tokens, other_tokens, full, other_d, gate, up):
    feature, units = gate.shape
    size = feature // GRAD_CHUNKS
    contract = (((0,), (0,)), ((), ()))
    for c in range(GRAD_CHUNKS):
        span = slice(c * size, (c + 1) * size)
        tokens = jnp.concatenate([own_tokens[:, span], other_tokens[:, span]], axis=0).T
        for k, out in enumerate((gate, up)):
            d = jnp.concatenate(
                [
                    full[:, k * units : (k + 1) * units],
                    other_d[:, k * units : (k + 1) * units],
                ],
                axis=0,
            )
            out[span] = jnp.dot(tokens, d, preferred_element_type=F32).astype(BF16)


def cost(rows, feature, columns):
    return pl.CostEstimate(
        flops=2 * rows * feature * columns,
        bytes_accessed=2 * feature * columns,
        transcendentals=0,
    )


def token_copies(tokens, peers):
    return pl.pallas_call(
        copies_kernel,
        out_shape=jax.ShapeDtypeStruct((peers,) + tokens.shape[1:], BF16),
        in_specs=[VMEM],
        out_specs=VMEM,
        compiler_params=PARAMS,
        name="copies",
    )(tokens)


def own_products(pieces, weights):
    peers, rows, feature = pieces.shape
    count, units = peers * rows, weights[0].shape[1]
    return pl.pallas_call(
        own_kernel,
        out_shape=(
            jax.ShapeDtypeStruct((count, feature), BF16),
            jax.ShapeDtypeStruct((count, 2 * units), BF16),
        ),
        in_specs=[HBM] * 3,
        out_specs=(VMEM, VMEM),
        scratch_shapes=[
            pltpu.VMEM(pieces.shape, BF16),
            pltpu.VMEM((2, feature, units), BF16),
            pltpu.SemaphoreType.DMA((3,)),
        ],
        compiler_params=FORWARD,
        cost_estimate=cost(8 * count, feature, 2 * units),
        name="own_products",
    )(pieces, *weights)


def other_products(flat, own, weights):
    count, feature = flat.shape
    units = weights[0].shape[1]
    return pl.pallas_call(
        other_kernel,
        out_shape=jax.ShapeDtypeStruct((count, 4 * units), BF16),
        in_specs=[VMEM] * 2 + [HBM] * 2,
        out_specs=VMEM,
        scratch_shapes=[
            pltpu.VMEM((2, feature, units), BF16),
            pltpu.SemaphoreType.DMA((2,)),
        ],
        compiler_params=PARAMS,
        cost_estimate=cost(count, feature, 2 * units),
        name="other_products",
    )(flat, own, *weights)


def hidden_and_gradients(received, cotangent):
    return pl.pallas_call(
        hidden_kernel,
        out_shape=(
            jax.ShapeDtypeStruct(cotangent.shape, BF16),
            jax.ShapeDtypeStruct(received.shape, BF16),
        ),
        in_specs=[VMEM] * 2,
        out_specs=(VMEM, VMEM),
        compiler_params=PARAMS,
        name="hidden_and_gradients",
    )(received, cotangent)


def input_blocks(full, weights, peers):
    count = full.shape[0]
    feature, units = weights[0].shape
    return pl.pallas_call(
        backward_kernel,
        out_shape=jax.ShapeDtypeStruct((peers, count * feature // peers // 128, 128), BF16),
        in_specs=[VMEM] + [HBM] * 4,
        out_specs=VMEM,
        scratch_shapes=[
            pltpu.VMEM((4, feature, units), BF16),
            pltpu.SemaphoreType.DMA((CHUNKS, 4)),
        ],
        compiler_params=BACKWARD,
        cost_estimate=cost(count, feature, 4 * units),
        name="input_blocks",
    )(full, *weights)


def gradients(own_tokens, other_tokens, full, other_d, units):
    feature = own_tokens.shape[1]
    shape = jax.ShapeDtypeStruct((feature, units), BF16)
    return pl.pallas_call(
        gradient_kernel,
        out_shape=(shape, shape),
        in_specs=[VMEM] * 4,
        out_specs=(VMEM, VMEM),
        compiler_params=PARAMS,
        cost_estimate=cost(own_tokens.shape[0], feature, 4 * units),
        name="gradients",
    )(own_tokens, other_tokens, full, other_d)


def per_device(tokens, gate_weight, up_weight, cotangent):
    rows, feature = tokens.shape[1], tokens.shape[2]
    units = gate_weight.shape[1]
    quarters = lax.axis_size("dep")
    micro = lax.axis_size("dp")
    lanes = lax.axis_size("out") * rows
    peers = lax.axis_size("x") * micro * lax.axis_size("out")
    first = lax.axis_index("core") == 0

    def swap(block):
        return lax.ppermute(block, "core", ((0, 1), (1, 0)))

    def paired(even, odd):
        return jnp.where(first, even, odd), jnp.where(first, odd, even)

    arrived = lax.all_to_all(token_copies(tokens, peers), CHIPS, 0, 0, tiled=True)

    own_weights = (gate_weight, up_weight)
    other_weights = (swap(gate_weight), swap(up_weight))
    own_tokens, own_partial = own_products(arrived, own_weights)
    partial = other_products(own_tokens, own_partial, other_weights)

    cot = cotangent.reshape(micro, 2, lanes, units)
    cot_own, cot_sent = paired(cot[:, 0], cot[:, 1])
    cot = jnp.concatenate([cot_own, swap(cot_sent)], axis=2).reshape(-1, 2 * units)

    received = lax.all_to_all(
        partial.reshape(quarters, -1, 4 * units), "dep", 0, 0, tiled=True
    )
    hidden, d_copies = hidden_and_gradients(received, cot)
    hidden = hidden.reshape(micro, lanes, 2 * units)
    full = lax.all_to_all(d_copies, "dep", 0, 0, tiled=True).reshape(-1, 4 * units)

    blocks = input_blocks(full, own_weights + other_weights, peers)
    pieces = lax.all_to_all(blocks, CHIPS, 0, 0, tiled=True)
    input_grad = jnp.sum(pieces.astype(F32), axis=0).astype(BF16)
    input_grad = input_grad.reshape(-1, rows, 128).swapaxes(0, 1)

    other_tokens = swap(own_tokens)
    other_d = swap(full[:, 2 * units :])
    gate_grad, up_grad = gradients(own_tokens, other_tokens, full, other_d, units)

    hid = paired(hidden[:, :, :units], swap(hidden[:, :, units:]))
    return (
        jnp.stack(hid, axis=1).reshape(cotangent.shape),
        input_grad.reshape(tokens.shape),
        gate_grad,
        up_grad,
    )


def solution(mesh):
    dp, inp, out, dep = (mesh.shape[name] for name in ("dp", "inp", "out", "dep"))
    split = Mesh(
        np.asarray(mesh.devices).reshape(dp, inp // 2, 2, out, dep),
        ("dp", "x", "core", "out", "dep"),
    )
    tokens_at = P("dp", ("x", "core", "out"), "dep")
    weight_at = P("dep", ("dp", "x", "core", "out"))
    hidden_at = P(None, "dep", ("dp", "x", "core", "out"))
    return jax.shard_map(
        per_device,
        mesh=split,
        in_specs=(tokens_at, weight_at, weight_at, hidden_at),
        out_specs=(hidden_at, tokens_at, weight_at, weight_at),
        check_vma=False,
    )
```

```python
import jax
import jax.numpy as jnp
import numpy as np
from jax import lax
from jax.experimental import pallas as pl
from jax.experimental.pallas import tpu as pltpu
from jax.sharding import Mesh, PartitionSpec as P

F32 = jnp.float32
BF16 = jnp.bfloat16
CHIPS = ("x", "dp", "out")


VMEM = pl.BlockSpec(memory_space=pltpu.VMEM)
HBM = pl.BlockSpec(memory_space=pltpu.HBM)
MIB = 1024 * 1024
PARAMS = pltpu.CompilerParams(vmem_limit_bytes=24 * MIB)
FORWARD = pltpu.CompilerParams(vmem_limit_bytes=51 * MIB + MIB // 2)
BACKWARD = pltpu.CompilerParams(vmem_limit_bytes=51 * MIB)
CHUNKS = 2
GRAD_CHUNKS = 4


def copies_kernel(tokens, copies, landed, arrived):
    fetched = pltpu.make_async_copy(tokens, landed, arrived.at[0])
    fetched.start()
    fetched.wait()
    copies[...] = jnp.broadcast_to(landed[...], copies.shape)


def own_kernel(pieces, w0, w1, flat, partial, landed, held, arrived):
    units = w0.shape[1]
    fetched = pltpu.make_async_copy(pieces, landed, arrived.at[2])
    copies = [
        pltpu.make_async_copy(w, held.at[k], arrived.at[k]) for k, w in enumerate((w0, w1))
    ]
    fetched.start()
    for copy in copies:
        copy.start()
    fetched.wait()
    flat[...] = landed[...].reshape(flat.shape)
    for k, copy in enumerate(copies):
        copy.wait()
        block = jnp.dot(flat[...], held[k], preferred_element_type=F32)
        partial[:, k * units : (k + 1) * units] = block.astype(BF16)


def other_kernel(flat, own, w0, w1, partial, held, arrived):
    units = w0.shape[1]
    copies = [
        pltpu.make_async_copy(w, held.at[k], arrived.at[k]) for k, w in enumerate((w0, w1))
    ]
    for copy in copies:
        copy.start()
    partial[:, : 2 * units] = own[...]
    for k, copy in enumerate(copies):
        copy.wait()
        block = jnp.dot(flat[...], held[k], preferred_element_type=F32)
        partial[:, (2 + k) * units : (3 + k) * units] = block.astype(BF16)


def hidden_kernel(received, cotangent, hidden, spread):
    units = cotangent.shape[1] // 2
    for h in range(2):
        at = slice(h * units, (h + 1) * units)
        gate_at = slice(2 * h * units, (2 * h + 1) * units)
        up_at = slice((2 * h + 1) * units, (2 * h + 2) * units)
        gate_vals = jnp.sum(received[:, :, gate_at].astype(F32), axis=0)
        up_vals = jnp.sum(received[:, :, up_at].astype(F32), axis=0)
        cot_vals = cotangent[:, at].astype(F32)
        sig_gate = jax.nn.sigmoid(gate_vals)
        silu_gate = gate_vals * sig_gate
        hidden[:, at] = (silu_gate * up_vals).astype(BF16)
        d_gate = cot_vals * up_vals * sig_gate * (1.0 + gate_vals * (1.0 - sig_gate))
        d_up = cot_vals * silu_gate
        for q in range(spread.shape[0]):
            spread[q, :, gate_at] = d_gate.astype(BF16)
            spread[q, :, up_at] = d_up.astype(BF16)


def backward_kernel(full, w0, w1, w2, w3, blocks, held, arrived):
    peers = blocks.shape[0]
    rows = full.shape[0] // peers
    feature, units = w0.shape
    size = feature // CHUNKS
    copies = [
        [
            pltpu.make_async_copy(
                w.at[pl.ds(c * size, size)], held.at[k, pl.ds(c * size, size)], arrived.at[c, k]
            )
            for k, w in enumerate((w0, w1, w2, w3))
        ]
        for c in range(CHUNKS)
    ]
    for copy in copies[0]:
        copy.start()
    for c, chunk in enumerate(copies):
        for copy in chunk:
            copy.wait()
        if c + 1 < CHUNKS:
            for copy in copies[c + 1]:
                copy.start()
        total = sum(
            lax.dot_general(
                full[:, k * units : (k + 1) * units],
                held[k, c * size : (c + 1) * size],
                (((1,), (1,)), ((), ())),
                preferred_element_type=F32,
            )
            for k in range(4)
        )
        for j in range(size // 128):
            at = (c * size // 128 + j) * rows
            tile = total[:, j * 128 : (j + 1) * 128].astype(BF16)
            blocks[:, at : at + rows, :] = tile.reshape(peers, rows, 128)


def gradient_kernel(own_tokens, other_tokens, full, other_d, gate, up):
    feature, units = gate.shape
    size = feature // GRAD_CHUNKS
    contract = (((0,), (0,)), ((), ()))
    for c in range(GRAD_CHUNKS):
        span = slice(c * size, (c + 1) * size)
        tokens = jnp.concatenate([own_tokens[:, span], other_tokens[:, span]], axis=0).T
        for k, out in enumerate((gate, up)):
            d = jnp.concatenate(
                [
                    full[:, k * units : (k + 1) * units],
                    other_d[:, k * units : (k + 1) * units],
                ],
                axis=0,
            )
            out[span] = jnp.dot(tokens, d, preferred_element_type=F32).astype(BF16)


def cost(rows, feature, columns):
    return pl.CostEstimate(
        flops=2 * rows * feature * columns,
        bytes_accessed=2 * feature * columns,
        transcendentals=0,
    )


def token_copies(tokens, peers):
    return pl.pallas_call(
        copies_kernel,
        out_shape=jax.ShapeDtypeStruct((peers,) + tokens.shape[1:], BF16),
        in_specs=[HBM],
        out_specs=VMEM,
        scratch_shapes=[pltpu.VMEM(tokens.shape, BF16), pltpu.SemaphoreType.DMA((1,))],
        compiler_params=pltpu.CompilerParams(vmem_limit_bytes=62 * MIB),
        name="copies",
    )(tokens)


def own_products(pieces, weights):
    peers, rows, feature = pieces.shape
    count, units = peers * rows, weights[0].shape[1]
    return pl.pallas_call(
        own_kernel,
        out_shape=(
            jax.ShapeDtypeStruct((count, feature), BF16),
            jax.ShapeDtypeStruct((count, 2 * units), BF16),
        ),
        in_specs=[HBM] * 3,
        out_specs=(VMEM, VMEM),
        scratch_shapes=[
            pltpu.VMEM(pieces.shape, BF16),
            pltpu.VMEM((2, feature, units), BF16),
            pltpu.SemaphoreType.DMA((3,)),
        ],
        compiler_params=FORWARD,
        cost_estimate=cost(8 * count, feature, 2 * units),
        name="own_products",
    )(pieces, *weights)


def other_products(flat, own, weights):
    count, feature = flat.shape
    units = weights[0].shape[1]
    return pl.pallas_call(
        other_kernel,
        out_shape=jax.ShapeDtypeStruct((count, 4 * units), BF16),
        in_specs=[VMEM] * 2 + [HBM] * 2,
        out_specs=VMEM,
        scratch_shapes=[
            pltpu.VMEM((2, feature, units), BF16),
            pltpu.SemaphoreType.DMA((2,)),
        ],
        compiler_params=PARAMS,
        cost_estimate=cost(count, feature, 2 * units),
        name="other_products",
    )(flat, own, *weights)


def hidden_and_gradients(received, cotangent):
    return pl.pallas_call(
        hidden_kernel,
        out_shape=(
            jax.ShapeDtypeStruct(cotangent.shape, BF16),
            jax.ShapeDtypeStruct(received.shape, BF16),
        ),
        in_specs=[VMEM] * 2,
        out_specs=(VMEM, VMEM),
        compiler_params=PARAMS,
        name="hidden_and_gradients",
    )(received, cotangent)


def input_blocks(full, weights, peers):
    count = full.shape[0]
    feature, units = weights[0].shape
    return pl.pallas_call(
        backward_kernel,
        out_shape=jax.ShapeDtypeStruct((peers, count * feature // peers // 128, 128), BF16),
        in_specs=[VMEM] + [HBM] * 4,
        out_specs=VMEM,
        scratch_shapes=[
            pltpu.VMEM((4, feature, units), BF16),
            pltpu.SemaphoreType.DMA((CHUNKS, 4)),
        ],
        compiler_params=BACKWARD,
        cost_estimate=cost(count, feature, 4 * units),
        name="input_blocks",
    )(full, *weights)


def gradients(own_tokens, other_tokens, full, other_d, units):
    feature = own_tokens.shape[1]
    shape = jax.ShapeDtypeStruct((feature, units), BF16)
    return pl.pallas_call(
        gradient_kernel,
        out_shape=(shape, shape),
        in_specs=[VMEM] * 4,
        out_specs=(VMEM, VMEM),
        compiler_params=PARAMS,
        cost_estimate=cost(own_tokens.shape[0], feature, 4 * units),
        name="gradients",
    )(own_tokens, other_tokens, full, other_d)


def per_device(tokens, gate_weight, up_weight, cotangent):
    rows, feature = tokens.shape[1], tokens.shape[2]
    units = gate_weight.shape[1]
    quarters = lax.axis_size("dep")
    micro = lax.axis_size("dp")
    lanes = lax.axis_size("out") * rows
    peers = lax.axis_size("x") * micro * lax.axis_size("out")
    first = lax.axis_index("core") == 0

    def swap(block):
        return lax.ppermute(block, "core", ((0, 1), (1, 0)))

    def paired(even, odd):
        return jnp.where(first, even, odd), jnp.where(first, odd, even)

    arrived = lax.all_to_all(token_copies(tokens, peers), CHIPS, 0, 0, tiled=True)

    own_weights = (gate_weight, up_weight)
    other_weights = (swap(gate_weight), swap(up_weight))
    own_tokens, own_partial = own_products(arrived, own_weights)
    partial = other_products(own_tokens, own_partial, other_weights)

    cot = cotangent.reshape(micro, 2, lanes, units)
    cot_own, cot_sent = paired(cot[:, 0], cot[:, 1])
    cot = jnp.concatenate([cot_own, swap(cot_sent)], axis=2).reshape(-1, 2 * units)

    received = lax.all_to_all(
        partial.reshape(quarters, -1, 4 * units), "dep", 0, 0, tiled=True
    )
    hidden, d_copies = hidden_and_gradients(received, cot)
    hidden = hidden.reshape(micro, lanes, 2 * units)
    full = lax.all_to_all(d_copies, "dep", 0, 0, tiled=True).reshape(-1, 4 * units)

    blocks = input_blocks(full, own_weights + other_weights, peers)
    pieces = lax.all_to_all(blocks, CHIPS, 0, 0, tiled=True)
    input_grad = jnp.sum(pieces.astype(F32), axis=0).astype(BF16)
    input_grad = input_grad.reshape(-1, rows, 128).swapaxes(0, 1)

    other_tokens = swap(own_tokens)
    other_d = swap(full[:, 2 * units :])
    gate_grad, up_grad = gradients(own_tokens, other_tokens, full, other_d, units)

    hid = paired(hidden[:, :, :units], swap(hidden[:, :, units:]))
    return (
        jnp.stack(hid, axis=1).reshape(cotangent.shape),
        input_grad.reshape(tokens.shape),
        gate_grad,
        up_grad,
    )


def solution(mesh):
    dp, inp, out, dep = (mesh.shape[name] for name in ("dp", "inp", "out", "dep"))
    split = Mesh(
        np.asarray(mesh.devices).reshape(dp, inp // 2, 2, out, dep),
        ("dp", "x", "core", "out", "dep"),
    )
    tokens_at = P("dp", ("x", "core", "out"), "dep")
    weight_at = P("dep", ("dp", "x", "core", "out"))
    hidden_at = P(None, "dep", ("dp", "x", "core", "out"))
    return jax.shard_map(
        per_device,
        mesh=split,
        in_specs=(tokens_at, weight_at, weight_at, hidden_at),
        out_specs=(hidden_at, tokens_at, weight_at, weight_at),
        check_vma=False,
    )
```
